256 devices in a mesh: grp: 2 (over core), tp: 16 (over x, y), tok: 8 (over z).
Axes of the slice: x: 4, y: 4, z: 8, core: 2. Of those that a mesh axis runs over, the one named last changes fastest.
Arguments:
- teacher_hidden: bfloat16 [256, 16384], P('tok', 'tp'), may hold values from -6 to 6
- teacher_gain: float32 [16384], replicated, may hold values from 0.25 to 1.75
- teacher_head: bfloat16 [16384, 65536], P(None, ('grp', 'tp', 'tok')), may hold values from -1 to 1
- student_hidden: bfloat16 [256, 4096], P('tok', 'tp'), may hold values from -6 to 6
- student_gain: float32 [4096], replicated, may hold values from 0.25 to 1.75
- student_head: bfloat16 [4096, 65536], P(None, ('grp', 'tp', 'tok')), may hold values from -1 to 1
- targets: int32 [256], replicated, may hold values from 0 to 65535
Outputs:
- loss: float32 [256], replicated
- d_student_head: bfloat16 [4096, 65536], P(None, ('grp', 'tp', 'tok'))
- d_student_hidden: bfloat16 [256, 4096], P(('tp', 'tok'))
- d_student_gain: float32 [4096], replicated
The draws below stay inside these ranges and needn't reach their ends.
All inputs are finite; a program needn't handle non-finite values.
Results may differ from the reference program's by a relative error of at most 0.0067.
Values may be sent and summed in bfloat16 or wider, within the bound.
No kernel may reach another device: no remote copies, remote signals or barrier semaphores. Data moves between devices by JAX's collectives and lax.ppermute only.
A program may use at most 64 MiB of HBM per device.

```python
import math
import jax
import jax.numpy as jnp
from jax import lax

DT = 16384
DS = 4096
VOCAB = 65536
TOKENS = 256


def draw_teacher_hidden(key, part):
    key = jax.random.fold_in(key, 1)
    base = jnp.clip(jax.random.normal(jax.random.fold_in(key, 4), (TOKENS, DT), jnp.float32), -6.0, 6.0)
    return base.astype(jnp.bfloat16)


def draw_student_hidden(key, part):
    key = jax.random.fold_in(key, 2)
    base = jnp.clip(jax.random.normal(jax.random.fold_in(key, 4), (TOKENS, DS), jnp.float32), -6.0, 6.0)
    return base.astype(jnp.bfloat16)


def draw_teacher_head(key, part):
    key = jax.random.fold_in(key, 3)
    deviation = 2.0 / math.sqrt(DT)
    base = jnp.clip(jax.random.normal(jax.random.fold_in(key, 4), (DT, VOCAB), jnp.float32), -6.0, 6.0) * deviation
    return base.astype(jnp.bfloat16)


def draw_student_head(key, part):
    key = jax.random.fold_in(key, 4)
    deviation = 2.0 / math.sqrt(DS)
    base = jnp.clip(jax.random.normal(jax.random.fold_in(key, 4), (DS, VOCAB), jnp.float32), -6.0, 6.0) * deviation
    return base.astype(jnp.bfloat16)


def plant(values, stream_key, smallest, high):
    longest = values.shape.index(max(values.shape))
    spots = []
    for shift in (0, 1):
        where = [jax.random.randint(jax.random.fold_in(stream_key, axis), (), 0, length) for axis, length in enumerate(values.shape)]
        where[longest] = (where[longest] + shift) % values.shape[longest]
        spots.append(tuple(where))
    return values.at[spots[0]].set(smallest).at[spots[1]].set(high)


def setup_inputs(seed: int = 0) -> dict:
    keys = jax.random.split(jax.random.key(seed), 8)
    teacher_hidden = draw_teacher_hidden(jax.random.fold_in(keys[7], 71), 0)
    teacher_gain = jnp.clip(1.0 + 0.15 * jax.random.normal(keys[1], (DT,), jnp.float32), 0.25, 1.75)
    teacher_head = draw_teacher_head(jax.random.fold_in(keys[7], 71), 0)
    student_hidden = draw_student_hidden(jax.random.fold_in(keys[7], 71), 0)
    student_gain = jnp.clip(1.0 + 0.15 * jax.random.normal(keys[4], (DS,), jnp.float32), 0.25, 1.75)
    student_head = draw_student_head(jax.random.fold_in(keys[7], 71), 0)
    targets = plant(jax.random.randint(keys[6], (TOKENS,), 0, VOCAB), jax.random.fold_in(keys[6], 1), 0, VOCAB - 1).astype(jnp.int32)
    return {"teacher_hidden": teacher_hidden, "teacher_gain": teacher_gain, "teacher_head": teacher_head, "student_hidden": student_hidden, "student_gain": student_gain, "student_head": student_head, "targets": targets}


EPS = 1e-05
ALPHA = 0.0625
LOSS_SCALE = 4096.0

def rms_norm(hidden, gain):
    input_values = hidden.astype(jnp.float32)
    inverse_rms_scale = lax.rsqrt(lax.optimization_barrier(jnp.mean(input_values * input_values, axis=1, keepdims=True)) + EPS)
    return (input_values * inverse_rms_scale * gain).astype(jnp.bfloat16)

def log_total(logits):
    top = lax.optimization_barrier(jnp.max(logits, axis=1))
    total = lax.optimization_barrier(jnp.sum(jnp.exp(logits - top[:, None]), axis=1))
    return top + jnp.log(total)

def reference(teacher_hidden, teacher_gain, teacher_head, student_hidden, student_gain, student_head, targets):
    teacher_normed = rms_norm(teacher_hidden, teacher_gain)
    teacher_logits = jnp.dot(teacher_normed, teacher_head, preferred_element_type=jnp.float32)
    student_normed = rms_norm(student_hidden, student_gain)
    student_logits = jnp.dot(student_normed, student_head, preferred_element_type=jnp.float32)
    lse_t = log_total(teacher_logits)
    lse_s = log_total(student_logits)
    log_t = teacher_logits - lse_t[:, None]
    log_s = student_logits - lse_s[:, None]
    p_t = jnp.exp(log_t)
    p_s = jnp.exp(log_s)
    columns = jnp.arange(student_logits.shape[1], dtype=jnp.int32)
    onehot = columns[None, :] == targets[:, None]
    target_logit = lax.optimization_barrier(jnp.sum(jnp.where(onehot, student_logits, jnp.float32(0.0)), axis=1))
    loss = lax.optimization_barrier(jnp.sum(p_t * (log_t - log_s), axis=1)) + ALPHA * (lse_s - target_logit)
    grad_logits = (LOSS_SCALE * ((1.0 + ALPHA) * p_s - p_t - ALPHA * onehot.astype(jnp.float32))).astype(jnp.bfloat16)
    d_head = lax.dot_general(student_normed, grad_logits, (((0,), (0,)), ((), ())), preferred_element_type=jnp.float32).astype(jnp.bfloat16)
    normed_gradient = lax.dot_general(grad_logits, student_head, (((1,), (1,)), ((), ())), preferred_element_type=jnp.float32)
    input_values = student_hidden.astype(jnp.float32)
    inverse_rms_scale = lax.rsqrt(lax.optimization_barrier(jnp.mean(input_values * input_values, axis=1, keepdims=True)) + EPS)
    normalized_input = input_values * inverse_rms_scale
    incoming_gradient = normed_gradient * student_gain
    hidden_gradient = (inverse_rms_scale * (incoming_gradient - normalized_input * lax.optimization_barrier(jnp.mean(incoming_gradient * normalized_input, axis=1, keepdims=True)))).astype(jnp.bfloat16)
    gain_gradient = lax.optimization_barrier(jnp.sum(normed_gradient * normalized_input, axis=0))
    return (loss, d_head, hidden_gradient, gain_gradient)
```

```python
import functools

import jax
import jax.numpy as jnp
from jax import lax
from jax.experimental import pallas as pl
from jax.experimental.pallas import tpu as pltpu
from jax.sharding import PartitionSpec as P

EPS = 1e-05
ALPHA = 0.0625
LOSS_SCALE = 4096.0
AXES = ("grp", "tp", "tok")
F32 = jnp.float32
BF16 = jnp.bfloat16
VMEM_LIMIT = 48 * 1024 * 1024
NX, NY, NZ = 4, 4, 8
NTP = NX * NY
TOKENS = 256
KT = 512
KS = 128
VOC = 256


def permute(value, move):
    pairs = []
    for g in range(2):
        for x in range(NX):
            for y in range(NY):
                for z in range(NZ):
                    g2, x2, y2, z2 = move(g, x, y, z)
                    source = (g * NTP + x * NY + y) * NZ + z
                    target = ((g2 % 2) * NTP + (x2 % NX) * NY + y2 % NY) * NZ + z2 % NZ
                    pairs.append((source, target))
    return lax.ppermute(value, AXES, pairs)


def swap_cores(value):
    return permute(value, lambda g, x, y, z: (g + 1, x, y, z))


def shift_z(value, d):
    return permute(value, lambda g, x, y, z: (g, x, y, z + d))


def shift_first(value, d):
    return permute(value, lambda g, x, y, z: (g, x, y + d, z) if g == 0 else (g, x + d, y, z))


def shift_second(value, d):
    return permute(value, lambda g, x, y, z: (g, x + d, y, z) if g == 0 else (g, x, y + d, z))


def params(limit=VMEM_LIMIT):
    return pltpu.CompilerParams(vmem_limit_bytes=limit)


def dot(a, b, dims):
    return lax.dot_general(a, b, (dims, ((), ())), preferred_element_type=F32)


def logits_kernel(
    where, own, back, fore, far_a, far_b, r_t, r_s, gain_t, gain_s, w_own, w_oth, s_own, s_oth,
    logits, normed_s, raw_s,
):
    j = pl.program_id(0)
    g = where[16]

    @pl.when(j == 0)
    def _():
        logits[...] = jnp.zeros_like(logits)

    def step(block):
        h_t = block[0, :, :KT].astype(F32)
        n_t = (h_t * r_t[...] * gain_t[0]).astype(BF16)
        h_s = block[0, :, KT:]
        n_s = (h_s.astype(F32) * r_s[...] * gain_s[0]).astype(BF16)
        normed_s[0] = n_s
        raw_s[0] = h_s
        mine = pl.ds(pl.multiple_of(g * VOC, VOC), VOC)
        other = pl.ds(pl.multiple_of((1 - g) * VOC, VOC), VOC)
        nn = ((1,), (0,))
        logits[0, :, mine] += dot(n_t, w_own[0, 0], nn)
        logits[0, :, other] += dot(n_t, w_oth[0], nn)
        logits[1, :, mine] += dot(n_s, s_own[0, 0], nn)
        logits[1, :, other] += dot(n_s, s_oth[0], nn)

    for ref, low, high in (
        (own, 0, 4), (back, 4, 8), (fore, 8, 12), (far_a, 12, 14), (far_b, 14, 16),
    ):
        pl.when((j >= low) & (j < high))(functools.partial(step, ref))


def partial_logits(where, pieces, r_t, r_s, gain_t, gain_s, w4, w_oth, s4, s_oth):
    def piece(low, count):
        return pl.BlockSpec(
            (1, TOKENS, KT + KS), lambda j, w: (jnp.clip(j - low, 0, count - 1), 0, 0)
        )

    column = pl.BlockSpec((TOKENS, 1), lambda j, w: (0, 0))
    grid_spec = pltpu.PrefetchScalarGridSpec(
        num_scalar_prefetch=1,
        grid=(16,),
        in_specs=[
            piece(0, 4), piece(4, 4), piece(8, 4), piece(12, 2), piece(14, 2), column, column,
            pl.BlockSpec((1, 1, KT), lambda j, w: (w[j] * 2 + w[16], 0, 0)),
            pl.BlockSpec((1, 1, KS), lambda j, w: (w[j] * 2 + w[16], 0, 0)),
            pl.BlockSpec((1, 1, KT, VOC), lambda j, w: (w[j], w[16], 0, 0)),
            pl.BlockSpec((1, KT, VOC), lambda j, w: (w[j], 0, 0)),
            pl.BlockSpec((1, 1, KS, VOC), lambda j, w: (w[j], w[16], 0, 0)),
            pl.BlockSpec((1, KS, VOC), lambda j, w: (w[j], 0, 0)),
        ],
        out_specs=[
            pl.BlockSpec((2, TOKENS, 2 * VOC), lambda j, w: (0, 0, 0)),
            pl.BlockSpec((1, TOKENS, KS), lambda j, w: (w[j], 0, 0)),
            pl.BlockSpec((1, TOKENS, KS), lambda j, w: (w[j], 0, 0)),
        ],
    )
    return pl.pallas_call(
        logits_kernel,
        grid_spec=grid_spec,
        out_shape=[
            jax.ShapeDtypeStruct((2, TOKENS, 2 * VOC), F32),
            jax.ShapeDtypeStruct((NTP, TOKENS, KS), BF16),
            jax.ShapeDtypeStruct((NTP, TOKENS, KS), BF16),
        ],
        compiler_params=params(),
    )(where, *pieces, r_t, r_s, gain_t, gain_s, w4, w_oth, s4, s_oth)


def onehot_of(targets, base):
    lane = lax.broadcasted_iota(jnp.int32, (TOKENS, 2 * VOC), 1)
    column = jnp.where(lane < VOC, base[0] + lane, base[1] + lane - VOC)
    return column == targets


def stats_kernel(base, mine, other, targets, both, records):
    t = mine[0] + other[0]
    s = mine[1] + other[1]
    both[0] = t
    both[1] = s

    def row_sum(v):
        return jnp.sum(v, axis=1, keepdims=True)

    m_t = jnp.max(t, axis=1, keepdims=True)
    m_s = jnp.max(s, axis=1, keepdims=True)
    e_t = jnp.exp(t - m_t)
    hit = onehot_of(targets[...], base)
    columns = [
        m_t, row_sum(e_t), row_sum(e_t * (t - s)), m_s, row_sum(jnp.exp(s - m_s)),
        row_sum(jnp.where(hit, s, 0.0)),
    ]
    lane = lax.broadcasted_iota(jnp.int32, (TOKENS, 128), 1)
    packed = jnp.zeros((TOKENS, 128), F32)
    for k, column in enumerate(columns):
        packed = jnp.where(lane == k, column, packed)
    rows = jnp.transpose(packed)[:8]
    for k in range(NTP):
        records[k] = rows


def local_stats(base, mine, other, targets):
    vmem = pl.BlockSpec(memory_space=pltpu.VMEM)
    return pl.pallas_call(
        stats_kernel,
        in_specs=[pl.BlockSpec(memory_space=pltpu.SMEM), vmem, vmem, vmem],
        out_specs=[vmem, vmem],
        out_shape=[
            jax.ShapeDtypeStruct((2, TOKENS, 2 * VOC), F32),
            jax.ShapeDtypeStruct((NTP, 8, TOKENS), F32),
        ],
        compiler_params=params(),
    )(base, mine, other, targets)


def merged(records):
    m_t, z_t, a, m_s, z_s, hit = (records[:, k, :] for k in range(6))
    top_t = jnp.max(m_t, axis=0, keepdims=True)
    top_s = jnp.max(m_s, axis=0, keepdims=True)
    w_t = jnp.exp(m_t - top_t)
    w_s = jnp.exp(m_s - top_s)

    def total(v):
        return jnp.sum(v, axis=0, keepdims=True)

    return top_t, total(w_t * z_t), total(w_t * a), top_s, total(w_s * z_s), total(hit)


def merge_kernel(copies, records, out):
    rows = merged(records[...])
    for c in range(copies):
        for k in range(6):
            out[c, k : k + 1, :] = rows[k]
        out[c, 6:8, :] = jnp.zeros((2, TOKENS), F32)


def merge_records(records, copies):
    vmem = pl.BlockSpec(memory_space=pltpu.VMEM)
    return pl.pallas_call(
        functools.partial(merge_kernel, copies),
        in_specs=[vmem],
        out_specs=vmem,
        out_shape=jax.ShapeDtypeStruct((copies, 8, TOKENS), F32),
        compiler_params=params(),
    )(records)


def grad_kernel(
    base, records, both, targets, r_s, raw_s, s_own, s_oth, parts, gain_hi, gain_lo, grad_own, loss, grads
):
    j = pl.program_id(0)
    g = base[2]

    @pl.when(j == 0)
    def _():
        top_t, z_t, a, top_s, z_s, hit = merged(records[...])
        lse_t = top_t + jnp.log(z_t)
        lse_s = top_s + jnp.log(z_s)
        loss[...] = a / z_t - lse_t + lse_s + ALPHA * (lse_s - hit)
        row = lax.broadcasted_iota(jnp.int32, (128, TOKENS), 0)
        packed = jnp.where(row == 0, lse_t, jnp.where(row == 1, lse_s, 0.0))
        columns = jnp.transpose(packed)
        p_t = jnp.exp(both[0] - columns[:, 0:1])
        p_s = jnp.exp(both[1] - columns[:, 1:2])
        hits = onehot_of(targets[...], base).astype(F32)
        grad = (LOSS_SCALE * ((1.0 + ALPHA) * p_s - p_t - ALPHA * hits)).astype(BF16)
        grads[0] = grad[:, :VOC]
        grads[1] = grad[:, VOC:]
        grad_own[...] = grads[g]

    nt = ((1,), (1,))
    for k in range(4):
        part = dot(grads[g], s_own[k, 0], nt) + dot(grads[1 - g], s_oth[k], nt)
        parts[:, k * 16 : (k + 1) * 16, :] = part.astype(BF16).reshape(NTP, 16, KS)
        xhat = raw_s[k].astype(F32) * r_s[...]
        gain = jnp.sum(part * xhat, axis=0, keepdims=True)
        high = gain.astype(BF16)
        gain_hi[k] = high
        gain_lo[k] = (gain - high.astype(F32)).astype(BF16)


def grad_parts(base, records, both, targets, r_s, raw_s, s4, s_oth):
    whole = lambda *shape: pl.BlockSpec(shape, lambda j, b: (0,) * len(shape))
    grid_spec = pltpu.PrefetchScalarGridSpec(
        num_scalar_prefetch=1,
        grid=(4,),
        in_specs=[
            whole(NZ, 8, TOKENS), whole(2, TOKENS, 2 * VOC), whole(TOKENS, 1), whole(TOKENS, 1),
            pl.BlockSpec((4, TOKENS, KS), lambda j, b: (j, 0, 0)),
            pl.BlockSpec((4, 1, KS, VOC), lambda j, b: (j, b[2], 0, 0)),
            pl.BlockSpec((4, KS, VOC), lambda j, b: (j, 0, 0)),
        ],
        out_specs=[
            pl.BlockSpec((NTP, 64, KS), lambda j, b: (0, j, 0)),
            pl.BlockSpec((4, 1, KS), lambda j, b: (j, 0, 0)),
            pl.BlockSpec((4, 1, KS), lambda j, b: (j, 0, 0)),
            whole(TOKENS, VOC), whole(1, TOKENS),
        ],
        scratch_shapes=[pltpu.VMEM((2, TOKENS, VOC), BF16)],
    )
    return pl.pallas_call(
        grad_kernel,
        grid_spec=grid_spec,
        out_shape=[
            jax.ShapeDtypeStruct((NTP, 256, KS), BF16),
            jax.ShapeDtypeStruct((NTP, 1, KS), BF16),
            jax.ShapeDtypeStruct((NTP, 1, KS), BF16),
            jax.ShapeDtypeStruct((TOKENS, VOC), BF16),
            jax.ShapeDtypeStruct((1, TOKENS), F32),
        ],
        compiler_params=params(),
    )(base, records, both, targets, r_s, raw_s, s4, s_oth)


def head_kernel(base, mine, other, grad, out):
    g = base[2]
    tn = ((0,), (0,))
    for k in range(4):
        out[k, g] = dot(mine[k], grad[...], tn).astype(BF16)
        out[k, 1 - g] = dot(other[k], grad[...], tn).astype(BF16)


def head_gradient(base, mine, other, grad):
    block = pl.BlockSpec((4, TOKENS, KS), lambda j, b: (j, 0, 0))
    grid_spec = pltpu.PrefetchScalarGridSpec(
        num_scalar_prefetch=1,
        grid=(4,),
        in_specs=[block, block, pl.BlockSpec((TOKENS, VOC), lambda j, b: (0, 0))],
        out_specs=pl.BlockSpec((4, 2, KS, VOC), lambda j, b: (j, 0, 0, 0)),
    )
    return pl.pallas_call(
        head_kernel,
        grid_spec=grid_spec,
        out_shape=jax.ShapeDtypeStruct((NTP, 2, KS, VOC), BF16),
        compiler_params=params(),
    )(base, mine, other, grad)


def fold_kernel(parts, out, total):
    acc = parts[0].astype(F32)
    for k in range(1, NTP):
        acc = acc + parts[k].astype(F32)
    total[...] = acc
    gain = total[256:272, :] + total[272:288, :]
    for z in range(NZ):
        for i in range(2):
            out[z, i * 16 : (i + 1) * 16, :] = total[pl.ds(2 * z + i, 16, stride=16), :]
        out[z, 32:48, :] = gain


def fold_parts(parts):
    vmem = pl.BlockSpec(memory_space=pltpu.VMEM)
    return pl.pallas_call(
        fold_kernel,
        in_specs=[vmem],
        out_specs=vmem,
        out_shape=jax.ShapeDtypeStruct((NZ, 48, KS), F32),
        scratch_shapes=[pltpu.VMEM((288, KS), F32)],
        compiler_params=params(),
    )(parts)


def sum_kernel(parts, rows, out):
    acc = parts[0]
    for k in range(1, NZ):
        acc = acc + parts[k]
    out[0:48, :] = acc
    out[48:80, :] = rows[...]


def sum_parts(parts, rows):
    vmem = pl.BlockSpec(memory_space=pltpu.VMEM)
    return pl.pallas_call(
        sum_kernel,
        in_specs=[vmem, vmem],
        out_specs=vmem,
        out_shape=jax.ShapeDtypeStruct((80, KS), F32),
        compiler_params=params(),
    )(parts, rows)


def norm_backward(halves, gain):
    def tokens(v):
        return v.reshape(2, 2, NTP, KS).transpose(1, 2, 0, 3).reshape(2, 2 * NTP * KS)

    normed_gradient = tokens(halves[:, 0:32])
    input_values = tokens(halves[:, 48:80])
    gain_gradient = halves[:, 32:48].transpose(1, 0, 2).reshape(2 * NTP * KS)
    scale = lax.rsqrt(jnp.mean(input_values * input_values, axis=1, keepdims=True) + EPS)
    xhat = input_values * scale
    dy = normed_gradient * gain
    hidden_gradient = scale * (dy - xhat * jnp.mean(dy * xhat, axis=1, keepdims=True))
    return hidden_gradient.astype(BF16), gain_gradient


def on_device(
    teacher_hidden, teacher_gain, teacher_head, student_hidden, student_gain, student_head, targets
):
    g = lax.axis_index("grp")
    tp = lax.axis_index("tp")
    z = lax.axis_index("tok")
    x, y = tp // NY, tp % NY

    w4 = teacher_head.reshape(NTP, 2, KT, VOC)
    s4 = student_head.reshape(NTP, 2, KS, VOC)
    w_oth = swap_cores(lax.dynamic_index_in_dim(w4, 1 - g, 1, keepdims=False))
    s_oth = swap_cores(lax.dynamic_index_in_dim(s4, 1 - g, 1, keepdims=False))

    rows = teacher_hidden.shape[0]
    block = jnp.concatenate(
        [
            lax.dynamic_slice_in_dim(teacher_hidden, g * KT, KT, 1),
            lax.dynamic_slice_in_dim(student_hidden, g * KS, KS, 1),
        ],
        axis=1,
    )
    by_shift = [block] + [shift_z(block, d) for d in range(1, NZ)]
    ahead = [by_shift[(-i) % NZ] for i in range(NZ)]
    slab = lax.dynamic_slice_in_dim(
        jnp.concatenate(ahead + ahead, axis=0), ((NZ - z) % NZ) * rows, TOKENS, 0
    )
    own = jnp.stack([slab] + [shift_first(slab, d) for d in (1, 2, 3)])
    back = shift_second(own, 1)
    fore = shift_second(own, -1)
    far_a = shift_second(back[:2], 1)
    far_b = shift_second(fore[2:], -1)
    pieces = (own, back, fore, far_a, far_b)

    def squares(low, high):
        total = 0.0
        for piece in pieces:
            v = piece[:, :, low:high].astype(F32)
            total = total + jnp.sum(v * v, axis=(0, 2))
        return total

    squares_half = jnp.stack([squares(0, KT), squares(KT, KT + KS)])
    squares_all = squares_half + swap_cores(squares_half)
    width = jnp.array([teacher_gain.shape[0], student_gain.shape[0]], F32)[:, None]
    scales = lax.rsqrt(squares_all / width + EPS)
    r_t, r_s = scales[0][:, None], scales[1][:, None]

    a_pos = jnp.where(g == 0, x, y)
    b_pos = jnp.where(g == 0, y, x)
    a_abs = (a_pos + jnp.array([0, -1, 1, 2], jnp.int32)[:, None]) % 4
    b_abs = (b_pos - jnp.arange(4, dtype=jnp.int32)[None, :]) % 4
    place = jnp.where(g == 0, a_abs * NY + b_abs, b_abs * NY + a_abs).reshape(16)
    where = jnp.concatenate([place, g[None]]).astype(jnp.int32)
    half, normed_s, raw_s = partial_logits(
        where, pieces, r_t, r_s, teacher_gain.reshape(32, 1, KT), student_gain.reshape(32, 1, KS),
        w4, w_oth, s4, s_oth,
    )
    normed_oth = swap_cores(normed_s)
    chip = (tp * NZ + z) * VOC
    base = jnp.stack([chip, NTP * NZ * VOC + chip, g]).astype(jnp.int32)
    targets_column = targets[:, None]
    both, records = local_stats(base, half, swap_cores(half), targets_column)
    records = lax.all_to_all(records, "tp", 0, 0, tiled=True)
    records = lax.all_to_all(merge_records(records, NZ), "tok", 0, 0, tiled=True)
    parts, gain_hi, gain_lo, grad_own, loss = grad_parts(
        base, records, both, targets_column, r_s, raw_s, s4, s_oth
    )
    d_head = head_gradient(base, normed_s, normed_oth, grad_own)

    gain_rows = jnp.concatenate([gain_hi[:, 0], gain_lo[:, 0]], axis=0)
    outgoing = jnp.concatenate(
        [parts, jnp.broadcast_to(gain_rows[None], (NTP, 32, KS))], axis=1
    )
    arrived = lax.all_to_all(outgoing, "tp", 0, 0, tiled=True)
    arrived = lax.all_to_all(fold_parts(arrived), "tok", 0, 0, tiled=True)
    hidden_rows = lax.dynamic_slice_in_dim(raw_s, tp * 16 + z * 2, 2, 1)
    hidden_rows = hidden_rows.astype(F32).transpose(1, 0, 2).reshape(32, KS)
    mine = sum_parts(arrived, hidden_rows)
    other = swap_cores(mine)
    halves = jnp.where(g == 0, jnp.stack([mine, other]), jnp.stack([other, mine]))
    hidden_gradient, gain_gradient = norm_backward(halves, student_gain)
    return (
        loss.reshape(TOKENS),
        d_head.reshape(student_head.shape),
        hidden_gradient,
        gain_gradient,
    )


def solution(mesh):
    placed = (
        P("tok", "tp"),
        P(),
        P(None, ("grp", "tp", "tok")),
        P("tok", "tp"),
        P(),
        P(None, ("grp", "tp", "tok")),
        P(),
    )
    return jax.shard_map(
        on_device,
        mesh=mesh,
        in_specs=placed,
        out_specs=(P(), P(None, ("grp", "tp", "tok")), P(("tp", "tok"), None), P()),
        check_vma=False,
    )
```

```python
import functools

import jax
import jax.numpy as jnp
from jax import lax
from jax.experimental import pallas as pl
from jax.experimental.pallas import tpu as pltpu
from jax.sharding import PartitionSpec as P

EPS = 1e-05
ALPHA = 0.0625
LOSS_SCALE = 4096.0
AXES = ("grp", "tp", "tok")
F32 = jnp.float32
BF16 = jnp.bfloat16
VMEM_LIMIT = 16 * 1024 * 1024
WIDE_LIMIT = 20 * 1024 * 1024
NX, NY, NZ = 4, 4, 8
NTP = NX * NY
TOKENS = 256
KT = 512
KS = 128
VOC = 256


def permute(value, move):
    pairs = []
    for g in range(2):
        for x in range(NX):
            for y in range(NY):
                for z in range(NZ):
                    g2, x2, y2, z2 = move(g, x, y, z)
                    source = (g * NTP + x * NY + y) * NZ + z
                    target = ((g2 % 2) * NTP + (x2 % NX) * NY + y2 % NY) * NZ + z2 % NZ
                    pairs.append((source, target))
    return lax.ppermute(value, AXES, pairs)


def swap_cores(value):
    return permute(value, lambda g, x, y, z: (g + 1, x, y, z))


def shift_first(value, d):
    return permute(value, lambda g, x, y, z: (g, x, y + d, z) if g == 0 else (g, x + d, y, z))


def shift_second(value, d):
    return permute(value, lambda g, x, y, z: (g, x + d, y, z) if g == 0 else (g, x, y + d, z))


def params(limit=VMEM_LIMIT):
    return pltpu.CompilerParams(vmem_limit_bytes=limit)


def dot(a, b, dims):
    return lax.dot_general(a, b, (dims, ((), ())), preferred_element_type=F32)


def bring_kernel(w4, s4, w_own, s_own, sems):
    g = lax.axis_index("grp")
    copies = [
        pltpu.make_async_copy(source.at[:, g], target, sems.at[i])
        for i, (source, target) in enumerate(((w4, w_own), (s4, s_own)))
    ]
    for c in copies:
        c.start()
    for c in copies:
        c.wait()


def bring_halves(w4, s4):
    vmem = pl.BlockSpec(memory_space=pltpu.VMEM)
    hbm = pl.BlockSpec(memory_space=pl.ANY)
    return pl.pallas_call(
        bring_kernel,
        in_specs=[hbm, hbm],
        out_specs=[vmem, vmem],
        out_shape=[
            jax.ShapeDtypeStruct((NTP, KT, VOC), BF16),
            jax.ShapeDtypeStruct((NTP, KS, VOC), BF16),
        ],
        scratch_shapes=[pltpu.SemaphoreType.DMA((2,))],
        compiler_params=params(),
    )(w4, s4)


def logits_kernel(offsets, first, *refs):
    refs = list(refs)
    take = lambda n: [refs.pop(0) for _ in range(n)]
    arrays = 2 * len(offsets)
    hidden = take(arrays)
    r_t, r_s, gain_t, gain_s, w_own, w_oth, s_own, s_oth = take(8)
    before = None if first else take(3)[0]
    logits, normed_s, raw_s, acc, h_buf, w_buf, s_buf, n_buf, t_buf, in_sem, out_sem, acc_sem = refs
    g = lax.axis_index("grp")
    tp = lax.axis_index("tp")
    x, y = lax.div(tp, NY), lax.rem(tp, NY)
    position, line = jnp.where(g == 0, x, y), jnp.where(g == 0, y, x)
    copy = pltpu.make_async_copy
    if not first:
        load = copy(before, acc, acc_sem)
        load.start()
    places, arriving, leaving = [], [], []
    for a in range(arrays):
        ahead = lax.rem(position + offsets[a // 2] + NX, NX)
        for k in range(2):
            order = lax.rem(line - (2 * (a % 2) + k) + NX, NX)
            place = jnp.where(g == 0, ahead * NY + order, order * NY + ahead)
            places.append(place)
            t_rows, s_rows = pl.ds(k * KT, KT), pl.ds(k * KS, KS)
            sources = (
                (hidden[a].at[k], h_buf.at[a, k]),
                (w_own.at[place], w_buf.at[a, 0, t_rows]),
                (w_oth.at[place, g], w_buf.at[a, 1, t_rows]),
                (s_own.at[place], s_buf.at[a, 0, s_rows]),
                (s_oth.at[place, g], s_buf.at[a, 1, s_rows]),
            )
            n = 2 * a + k
            arriving.append([copy(p, q, in_sem.at[n, i]) for i, (p, q) in enumerate(sources)])
            for c in arriving[n]:
                c.start()
    for a in range(arrays):
        for k in range(2):
            n = 2 * a + k
            place = places[n]
            for c in arriving[n]:
                c.wait()
            row = pl.ds(place * 2 + g, 1)
            h_t = h_buf[a, k, :, :KT].astype(F32)
            t_buf[a, :, k * KT : (k + 1) * KT] = (h_t * r_t[...] * gain_t[row, :]).astype(BF16)
            h_s = h_buf[a, k, :, KT:].astype(F32)
            n_buf[a, :, k * KS : (k + 1) * KS] = (h_s * r_s[...] * gain_s[row, :]).astype(BF16)
            pairs = (
                (n_buf.at[a, :, pl.ds(k * KS, KS)], normed_s.at[place]),
                (h_buf.at[a, k, :, pl.ds(KT, KS)], raw_s.at[place]),
            )
            leaving.append([copy(p, q, out_sem.at[n, i]) for i, (p, q) in enumerate(pairs)])
            for c in leaving[n]:
                c.start()
        if a == 0 and not first:
            load.wait()
        nn = ((1,), (0,))
        for i, c in ((0, g), (1, 1 - g)):
            t = dot(t_buf[a], w_buf[a, i], nn)
            s = dot(n_buf[a], s_buf[a, i], nn)
            if a == 0 and first:
                acc[c, 0] = t
                acc[c, 1] = s
            else:
                acc[c, 0] += t
                acc[c, 1] += s
    store = copy(acc, logits, acc_sem)
    store.start()
    for copies in leaving:
        for c in copies:
            c.wait()
    store.wait()


def partial_logits(offsets, hidden, scales, gains, weights, before):
    first = before is None
    arrays = 2 * len(offsets)
    vmem = pl.BlockSpec(memory_space=pltpu.VMEM)
    hbm = pl.BlockSpec(memory_space=pl.ANY)
    out = pl.BlockSpec(memory_space=pltpu.HBM)
    operands = [*hidden, *scales, *gains, *weights]
    in_specs = [*[hbm] * arrays, *[vmem] * 4, *[hbm] * 4]
    aliases = {}
    if not first:
        aliases = {len(operands) + 1: 1, len(operands) + 2: 2}
        operands += before
        in_specs += [out] * 3
    return pl.pallas_call(
        functools.partial(logits_kernel, offsets, first),
        in_specs=in_specs,
        out_specs=[out] * 3,
        out_shape=[
            jax.ShapeDtypeStruct((2, 2, TOKENS, VOC), F32),
            jax.ShapeDtypeStruct((NTP, TOKENS, KS), BF16),
            jax.ShapeDtypeStruct((NTP, TOKENS, KS), BF16),
        ],
        scratch_shapes=[
            pltpu.VMEM((2, 2, TOKENS, VOC), F32),
            pltpu.VMEM((arrays, 2, TOKENS, KT + KS), BF16),
            pltpu.VMEM((arrays, 2, 2 * KT, VOC), BF16),
            pltpu.VMEM((arrays, 2, 2 * KS, VOC), BF16),
            pltpu.VMEM((arrays, TOKENS, 2 * KS), BF16),
            pltpu.VMEM((arrays, TOKENS, 2 * KT), BF16),
            pltpu.SemaphoreType.DMA((2 * arrays, 5)),
            pltpu.SemaphoreType.DMA((2 * arrays, 2)),
            pltpu.SemaphoreType.DMA,
        ],
        input_output_aliases=aliases,
        cost_estimate=pl.CostEstimate(
            flops=4 * arrays * TOKENS * 2 * VOC * (KT + KS),
            bytes_accessed=arrays * 2_400_000,
            transcendentals=0,
        ),
        compiler_params=params(WIDE_LIMIT),
    )(*operands)


def onehot_of(targets, base):
    spread = jnp.broadcast_to(targets.astype(F32), (128, TOKENS))
    targets = jnp.transpose(spread)[:, 0:1].astype(jnp.int32)
    lane = lax.broadcasted_iota(jnp.int32, (TOKENS, 2 * VOC), 1)
    column = jnp.where(lane < VOC, base[0] + lane, base[1] + lane - VOC)
    return column == targets


def stats_kernel(base, mine, other, targets, both, records):
    t, s = (
        jnp.concatenate([mine[0, i] + other[0, i], mine[1, i] + other[1, i]], axis=1)
        for i in range(2)
    )
    both[0] = t
    both[1] = s

    def row_sum(v):
        return jnp.sum(v, axis=1, keepdims=True)

    m_t = jnp.max(t, axis=1, keepdims=True)
    m_s = jnp.max(s, axis=1, keepdims=True)
    e_t = jnp.exp(t - m_t)
    hit = onehot_of(targets[...], base)
    columns = [
        m_t, row_sum(e_t), row_sum(e_t * (t - s)), m_s, row_sum(jnp.exp(s - m_s)),
        row_sum(jnp.where(hit, s, 0.0)),
    ]
    lane = lax.broadcasted_iota(jnp.int32, (TOKENS, 128), 1)
    packed = jnp.zeros((TOKENS, 128), F32)
    for k, column in enumerate(columns):
        packed = jnp.where(lane == k, column, packed)
    rows = jnp.transpose(packed)[:8]
    for k in range(NTP):
        records[k] = rows


def local_stats(base, mine, other, targets):
    vmem = pl.BlockSpec(memory_space=pltpu.VMEM)
    return pl.pallas_call(
        stats_kernel,
        in_specs=[pl.BlockSpec(memory_space=pltpu.SMEM), vmem, vmem, vmem],
        out_specs=[vmem, vmem],
        out_shape=[
            jax.ShapeDtypeStruct((2, TOKENS, 2 * VOC), F32),
            jax.ShapeDtypeStruct((NTP, 8, TOKENS), F32),
        ],
        compiler_params=params(),
    )(base, mine, other, targets)


def merged(records):
    m_t, z_t, a, m_s, z_s, hit = (records[:, k, :] for k in range(6))
    top_t = jnp.max(m_t, axis=0, keepdims=True)
    top_s = jnp.max(m_s, axis=0, keepdims=True)
    w_t = jnp.exp(m_t - top_t)
    w_s = jnp.exp(m_s - top_s)

    def total(v):
        return jnp.sum(v, axis=0, keepdims=True)

    return top_t, total(w_t * z_t), total(w_t * a), top_s, total(w_s * z_s), total(hit)


def merge_kernel(copies, records, out):
    rows = merged(records[...])
    for c in range(copies):
        for k in range(6):
            out[c, k : k + 1, :] = rows[k]
        out[c, 6:8, :] = jnp.zeros((2, TOKENS), F32)


def merge_records(records, copies):
    vmem = pl.BlockSpec(memory_space=pltpu.VMEM)
    return pl.pallas_call(
        functools.partial(merge_kernel, copies),
        in_specs=[vmem],
        out_specs=vmem,
        out_shape=jax.ShapeDtypeStruct((copies, 8, TOKENS), F32),
        compiler_params=params(),
    )(records)


def grad_kernel(
    base, records, both, targets, r_s, raw_s, s_own, s_oth, out, grad_own, loss, grads, gains, parts, sems
):
    j = pl.program_id(0)
    g = base[2]

    @pl.when(j == 0)
    def _():
        top_t, z_t, a, top_s, z_s, hit = merged(records[...])
        lse_t = top_t + jnp.log(z_t)
        lse_s = top_s + jnp.log(z_s)
        loss[...] = a / z_t - lse_t + lse_s + ALPHA * (lse_s - hit)
        row = lax.broadcasted_iota(jnp.int32, (128, TOKENS), 0)
        packed = jnp.where(row == 0, lse_t, jnp.where(row == 1, lse_s, 0.0))
        columns = jnp.transpose(packed)
        p_t = jnp.exp(both[0] - columns[:, 0:1])
        p_s = jnp.exp(both[1] - columns[:, 1:2])
        hits = onehot_of(targets[...], base).astype(F32)
        grad = (LOSS_SCALE * ((1.0 + ALPHA) * p_s - p_t - ALPHA * hits)).astype(BF16)
        grads[0] = grad[:, :VOC]
        grads[1] = grad[:, VOC:]
        grad_own[...] = grads[g]

    nt = ((1,), (1,))
    wide = (4 * KS, VOC)
    part = dot(grads[g], s_own[...].reshape(wide), nt) + dot(grads[1 - g], s_oth[...].reshape(wide), nt)
    for k in range(4):
        piece = part[:, k * KS : (k + 1) * KS]
        rows = pl.ds(pl.multiple_of((j * 4 + k) * 16, 16), 16)
        parts[:, rows, :] = piece.astype(BF16).reshape(NTP, 16, KS)
        xhat = raw_s[k].astype(F32) * r_s[...]
        gains[pl.ds(j * 4 + k, 1), :] = jnp.sum(piece * xhat, axis=0, keepdims=True)

    def leave(n, count):
        rows = pl.ds(pl.multiple_of(n * 64, 64), count)
        return pltpu.make_async_copy(parts.at[:, rows, :], out.at[:, rows, :], sems.at[n])

    leave(j, 64).start()

    @pl.when(j == 3)
    def _():
        gain = gains[...]
        high = gain.astype(BF16)
        low = (gain - high.astype(F32)).astype(BF16)
        for c in range(NTP):
            parts[c, 256:272, :] = high
            parts[c, 272:288, :] = low
        leave(4, 32).start()
        for n in range(4):
            leave(n, 64).wait()
        leave(4, 32).wait()


def grad_parts(base, records, both, targets, r_s, raw_s, s_own, s_oth):
    whole = lambda *shape: pl.BlockSpec(shape, lambda j, b: (0,) * len(shape))
    grid_spec = pltpu.PrefetchScalarGridSpec(
        num_scalar_prefetch=1,
        grid=(4,),
        in_specs=[
            whole(NZ, 8, TOKENS), whole(2, TOKENS, 2 * VOC), whole(1, TOKENS), whole(TOKENS, 1),
            pl.BlockSpec((4, TOKENS, KS), lambda j, b: (j, 0, 0)),
            pl.BlockSpec((4, KS, VOC), lambda j, b: (j, 0, 0)),
            pl.BlockSpec((4, 1, KS, VOC), lambda j, b: (j, b[2], 0, 0)),
        ],
        out_specs=[
            pl.BlockSpec(memory_space=pltpu.HBM), whole(TOKENS, VOC), whole(1, TOKENS),
        ],
        scratch_shapes=[
            pltpu.VMEM((2, TOKENS, VOC), BF16),
            pltpu.VMEM((NTP, KS), F32),
            pltpu.VMEM((NTP, 288, KS), BF16),
            pltpu.SemaphoreType.DMA((5,)),
        ],
    )
    return pl.pallas_call(
        grad_kernel,
        grid_spec=grid_spec,
        out_shape=[
            jax.ShapeDtypeStruct((NTP, 288, KS), BF16),
            jax.ShapeDtypeStruct((TOKENS, VOC), BF16),
            jax.ShapeDtypeStruct((1, TOKENS), F32),
        ],
        compiler_params=params(),
    )(base, records, both, targets, r_s, raw_s, s_own, s_oth)


def head_kernel(base, mine, other, grad, out):
    g = base[2]
    tn = ((0,), (0,))
    for k in range(4):
        out[k, g] = dot(mine[k], grad[...], tn).astype(BF16)
        out[k, 1 - g] = dot(other[k], grad[...], tn).astype(BF16)


def head_gradient(base, mine, other, grad):
    block = pl.BlockSpec((4, TOKENS, KS), lambda j, b: (j, 0, 0))
    grid_spec = pltpu.PrefetchScalarGridSpec(
        num_scalar_prefetch=1,
        grid=(4,),
        in_specs=[block, block, pl.BlockSpec((TOKENS, VOC), lambda j, b: (0, 0))],
        out_specs=pl.BlockSpec((4, 2, KS, VOC), lambda j, b: (j, 0, 0, 0)),
    )
    return pl.pallas_call(
        head_kernel,
        grid_spec=grid_spec,
        out_shape=jax.ShapeDtypeStruct((NTP, 2, KS, VOC), BF16),
        cost_estimate=pl.CostEstimate(
            flops=2 * NTP * 2 * KS * TOKENS * VOC, bytes_accessed=4_500_000, transcendentals=0
        ),
        compiler_params=params(),
    )(base, mine, other, grad)


def fold_kernel(parts, out, total):
    acc = parts[0].astype(F32)
    for k in range(1, NTP):
        acc = acc + parts[k].astype(F32)
    total[...] = acc
    gain = total[256:272, :] + total[272:288, :]
    for z in range(NZ):
        for i in range(2):
            out[z, i * 16 : (i + 1) * 16, :] = total[pl.ds(2 * z + i, 16, stride=16), :]
        out[z, 32:48, :] = gain


def fold_parts(parts):
    vmem = pl.BlockSpec(memory_space=pltpu.VMEM)
    return pl.pallas_call(
        fold_kernel,
        in_specs=[vmem],
        out_specs=vmem,
        out_shape=jax.ShapeDtypeStruct((NZ, 48, KS), F32),
        scratch_shapes=[pltpu.VMEM((288, KS), F32)],
        compiler_params=params(),
    )(parts)


def sum_kernel(parts, rows, out):
    acc = parts[0]
    for k in range(1, NZ):
        acc = acc + parts[k]
    out[0:48, :] = acc
    out[48:80, :] = rows[...]


def sum_parts(parts, rows):
    vmem = pl.BlockSpec(memory_space=pltpu.VMEM)
    return pl.pallas_call(
        sum_kernel,
        in_specs=[vmem, vmem],
        out_specs=vmem,
        out_shape=jax.ShapeDtypeStruct((80, KS), F32),
        compiler_params=params(),
    )(parts, rows)


def final_kernel(mine, other, gain, hidden, gain_gradient, rows):
    g = lax.axis_index("grp")

    def all_features(v):
        return jnp.sum(v)

    halves = (mine, other)
    total = []
    for i in range(2):
        own_rows = slice(48 + 16 * i, 64 + 16 * i)
        squares = sum(all_features(h[own_rows, :] * h[own_rows, :]) for h in halves)
        scale = lax.rsqrt(jnp.full((1, 1), squares / (2 * NTP * KS) + EPS, F32))
        pairs = []
        for k, h in enumerate(halves):
            xhat = h[own_rows, :] * scale
            dy = h[16 * i : 16 * i + 16, :] * gain[g if k == 0 else 1 - g]
            pairs.append((xhat, dy))
        mean = sum(all_features(dy * xhat) for xhat, dy in pairs) / (2 * NTP * KS)
        total.append([scale * (dy - xhat * mean) for xhat, dy in pairs])
    for k, h in enumerate(halves):
        c = g if k == 0 else 1 - g
        for j in range(NTP):
            lanes = pl.ds(pl.multiple_of((2 * j + c) * KS, KS), KS)
            for i in range(2):
                rows[i : i + 1, lanes] = total[i][k][j : j + 1, :]
            gain_gradient[:, lanes] = h[32 + j : 33 + j, :]
    hidden[...] = rows[0:2, :].astype(BF16)


def norm_backward(mine, other, gain):
    vmem = pl.BlockSpec(memory_space=pltpu.VMEM)
    return pl.pallas_call(
        final_kernel,
        in_specs=[vmem] * 3,
        out_specs=[vmem] * 2,
        out_shape=[
            jax.ShapeDtypeStruct((2, 2 * NTP * KS), BF16),
            jax.ShapeDtypeStruct((1, 2 * NTP * KS), F32),
        ],
        scratch_shapes=[pltpu.VMEM((8, 2 * NTP * KS), F32)],
        compiler_params=params(),
    )(mine, other, gain)


def squares_kernel(slab, out):
    def lanes(low, high):
        total = 0.0
        for k in range(low, high, 128):
            v = slab[:, k : k + 128].astype(F32)
            total = total + v * v
        return jnp.sum(jnp.transpose(total), axis=0, keepdims=True)

    out[0:1, :] = lanes(0, KT)
    out[1:2, :] = lanes(KT, KT + KS)
    out[2:8, :] = jnp.zeros((6, TOKENS), F32)


def both_kernel(mine, other, out):
    total = mine[...] + other[...]
    for k in range(NTP):
        out[k] = total


def scales_kernel(widths, squares, r_t, r_s):
    total = jnp.sum(squares[...], axis=0)
    columns = jnp.transpose(
        jnp.concatenate(
            [lax.rsqrt(total[i : i + 1, :] / widths[i] + EPS) for i in range(2)]
            + [jnp.zeros((126, TOKENS), F32)],
            axis=0,
        )
    )
    r_t[...] = columns[:, 0:1]
    r_s[...] = columns[:, 1:2]


def small_call(kernel, shapes, *operands):
    vmem = pl.BlockSpec(memory_space=pltpu.VMEM)
    return pl.pallas_call(
        kernel,
        in_specs=[vmem] * len(operands),
        out_specs=[vmem] * len(shapes),
        out_shape=[jax.ShapeDtypeStruct(shape, F32) for shape in shapes],
        compiler_params=params(),
    )(*operands)


def on_device(
    teacher_hidden, teacher_gain, teacher_head, student_hidden, student_gain, student_head, targets
):
    g = lax.axis_index("grp")
    tp = lax.axis_index("tp")
    z = lax.axis_index("tok")

    w4 = teacher_head.reshape(NTP, 2, KT, VOC)
    s4 = student_head.reshape(NTP, 2, KS, VOC)
    w_oth, s_oth = swap_cores(w4), swap_cores(s4)

    block = jnp.concatenate(
        [
            lax.dynamic_slice_in_dim(teacher_hidden, g * KT, KT, 1),
            lax.dynamic_slice_in_dim(student_hidden, g * KS, KS, 1),
        ],
        axis=1,
    )
    slab = lax.all_to_all(
        jnp.broadcast_to(block[None], (NZ, *block.shape)), "tok", 0, 0, tiled=True
    ).reshape(TOKENS, KT + KS)
    w_own, s_own = bring_halves(w4, s4)
    gain_t, gain_s = teacher_gain.reshape(32, KT), student_gain.reshape(32, KS)
    slab, w_oth, s_oth, w_own, s_own, gain_t, gain_s = lax.optimization_barrier(
        (slab, w_oth, s_oth, w_own, s_own, gain_t, gain_s)
    )
    by_shift = [shift_first(slab, d) for d in (1, 2, 3)]
    (half,) = small_call(squares_kernel, [(8, TOKENS)], slab)
    (copies,) = small_call(both_kernel, [(NTP, 8, TOKENS)], half, swap_cores(half))
    widths = (teacher_gain.shape[0], student_gain.shape[0])
    r_t, r_s = small_call(
        functools.partial(scales_kernel, widths),
        [(TOKENS, 1), (TOKENS, 1)],
        lax.all_to_all(copies, "tp", 0, 0, tiled=True),
    )
    low, high = jnp.stack([slab, by_shift[0]]), jnp.stack(by_shift[1:])
    low, high, r_t, r_s = lax.optimization_barrier((low, high, r_t, r_s))
    back_low = shift_second(low, 1)
    fore_high = shift_second(high, -1)
    back_high = shift_second(high, 1)
    fore_low = shift_second(low, -1)
    heads = functools.partial(
        partial_logits,
        scales=(r_t, r_s),
        gains=(gain_t, gain_s),
        weights=(w_own, w_oth, s_own, s_oth),
    )
    done = heads((0,), (low, high), before=None)
    *done, back_low, fore_high = lax.optimization_barrier((*done, back_low, fore_high))
    far_low = shift_second(back_low, 1)
    far_high = shift_second(fore_high, -1)
    done = heads((-1, 1), (back_low, back_high, fore_low, fore_high), before=done)
    half, normed_s, raw_s = heads((2,), (far_low, far_high), before=done)
    column = (tp * NZ + z) * VOC
    base = jnp.stack([column, NTP * NZ * VOC + column, g]).astype(jnp.int32)
    targets_row = targets[None, :]
    both, records = local_stats(base, half, swap_cores(half), targets_row)
    normed_oth = swap_cores(normed_s)
    records, normed_oth = lax.optimization_barrier((records, normed_oth))
    records = lax.all_to_all(records, "tp", 0, 0, tiled=True)
    records = lax.all_to_all(merge_records(records, NZ), "tok", 0, 0, tiled=True)
    parts, grad_own, loss = grad_parts(
        base, records, both, targets_row, r_s, raw_s, s_own, s_oth
    )
    arrived = lax.all_to_all(parts, "tp", 0, 0, tiled=True)
    d_head = head_gradient(base, normed_s, normed_oth, grad_own)
    arrived, d_head = lax.optimization_barrier((arrived, d_head))
    arrived = lax.all_to_all(fold_parts(arrived), "tok", 0, 0, tiled=True)
    hidden_rows = lax.dynamic_slice_in_dim(raw_s, tp * 16 + z * 2, 2, 1)
    hidden_rows = hidden_rows.astype(F32).transpose(1, 0, 2).reshape(32, KS)
    mine = sum_parts(arrived, hidden_rows)
    hidden_gradient, gain_gradient = norm_backward(
        mine, swap_cores(mine), student_gain.reshape(NTP, 2, KS).transpose(1, 0, 2)
    )
    return (
        loss.reshape(TOKENS),
        d_head.reshape(student_head.shape),
        hidden_gradient,
        gain_gradient.reshape(2 * NTP * KS),
    )


def solution(mesh):
    placed = (
        P("tok", "tp"),
        P(),
        P(None, ("grp", "tp", "tok")),
        P("tok", "tp"),
        P(),
        P(None, ("grp", "tp", "tok")),
        P(),
    )
    return jax.shard_map(
        on_device,
        mesh=mesh,
        in_specs=placed,
        out_specs=(P(), P(None, ("grp", "tp", "tok")), P(("tp", "tok"), None), P()),
        check_vma=False,
    )
```

```python
import functools

import jax
import jax.numpy as jnp
from jax import lax
from jax.experimental import pallas as pl
from jax.experimental.pallas import tpu as pltpu
from jax.sharding import PartitionSpec as P

EPS = 1e-05
ALPHA = 0.0625
LOSS_SCALE = 4096.0
AXES = ("grp", "tp", "tok")
F32 = jnp.float32
BF16 = jnp.bfloat16
VMEM_LIMIT = 16 * 1024 * 1024
WIDE_LIMIT = 20 * 1024 * 1024
NX, NY, NZ = 4, 4, 8
NTP = NX * NY
TOKENS = 256
KT = 512
KS = 128
VOC = 256


def permute(value, move):
    pairs = []
    for g in range(2):
        for x in range(NX):
            for y in range(NY):
                for z in range(NZ):
                    g2, x2, y2, z2 = move(g, x, y, z)
                    source = (g * NTP + x * NY + y) * NZ + z
                    target = ((g2 % 2) * NTP + (x2 % NX) * NY + y2 % NY) * NZ + z2 % NZ
                    pairs.append((source, target))
    return lax.ppermute(value, AXES, pairs)


def swap_cores(value):
    return permute(value, lambda g, x, y, z: (g + 1, x, y, z))


def shift_first(value, d):
    return permute(value, lambda g, x, y, z: (g, x, y + d, z) if g == 0 else (g, x + d, y, z))


def shift_second(value, d):
    return permute(value, lambda g, x, y, z: (g, x + d, y, z) if g == 0 else (g, x, y + d, z))


def params(limit=VMEM_LIMIT):
    return pltpu.CompilerParams(vmem_limit_bytes=limit)


def dot(a, b, dims):
    return lax.dot_general(a, b, (dims, ((), ())), preferred_element_type=F32)


def bring_kernel(w4, s4, w_own, s_own, sems):
    g = lax.axis_index("grp")
    copies = [
        pltpu.make_async_copy(source.at[:, g], target, sems.at[i])
        for i, (source, target) in enumerate(((w4, w_own), (s4, s_own)))
    ]
    for c in copies:
        c.start()
    for c in copies:
        c.wait()


def bring_halves(w4, s4):
    vmem = pl.BlockSpec(memory_space=pltpu.VMEM)
    hbm = pl.BlockSpec(memory_space=pl.ANY)
    return pl.pallas_call(
        bring_kernel,
        in_specs=[hbm, hbm],
        out_specs=[vmem, vmem],
        out_shape=[
            jax.ShapeDtypeStruct((NTP, KT, VOC), BF16),
            jax.ShapeDtypeStruct((NTP, KS, VOC), BF16),
        ],
        scratch_shapes=[pltpu.SemaphoreType.DMA((2,))],
        compiler_params=params(),
    )(w4, s4)


def logits_kernel(offsets, first, *refs):
    refs = list(refs)
    take = lambda n: [refs.pop(0) for _ in range(n)]
    arrays = 2 * len(offsets)
    hidden = take(arrays)
    r_t, r_s, gain_t, gain_s, w_own, w_oth, s_own, s_oth = take(8)
    before = None if first else take(3)[0]
    logits, normed_s, raw_s, acc, h_buf, w_buf, s_buf, n_buf, t_buf, in_sem, out_sem, acc_sem = refs
    g = lax.axis_index("grp")
    tp = lax.axis_index("tp")
    x, y = lax.div(tp, NY), lax.rem(tp, NY)
    position, line = jnp.where(g == 0, x, y), jnp.where(g == 0, y, x)
    copy = pltpu.make_async_copy
    if not first:
        load = copy(before, acc, acc_sem)
        load.start()
    places, arriving, leaving = [], [], []
    for a in range(arrays):
        ahead = lax.rem(position + offsets[a // 2] + NX, NX)
        for k in range(2):
            order = lax.rem(line - (2 * (a % 2) + k) + NX, NX)
            place = jnp.where(g == 0, ahead * NY + order, order * NY + ahead)
            places.append(place)
            t_rows, s_rows = pl.ds(k * KT, KT), pl.ds(k * KS, KS)
            sources = (
                (hidden[a].at[k], h_buf.at[a, k]),
                (w_own.at[place], w_buf.at[a, 0, t_rows]),
                (w_oth.at[place, g], w_buf.at[a, 1, t_rows]),
                (s_own.at[place], s_buf.at[a, 0, s_rows]),
                (s_oth.at[place, g], s_buf.at[a, 1, s_rows]),
            )
            n = 2 * a + k
            arriving.append([copy(p, q, in_sem.at[n, i]) for i, (p, q) in enumerate(sources)])
            for c in arriving[n]:
                c.start()
    for a in range(arrays):
        for k in range(2):
            n = 2 * a + k
            place = places[n]
            for c in arriving[n]:
                c.wait()
            row = pl.ds(place * 2 + g, 1)
            h_t = h_buf[a, k, :, :KT].astype(F32)
            t_buf[a, :, k * KT : (k + 1) * KT] = (h_t * r_t[...] * gain_t[row, :]).astype(BF16)
            h_s = h_buf[a, k, :, KT:].astype(F32)
            n_buf[a, :, k * KS : (k + 1) * KS] = (h_s * r_s[...] * gain_s[row, :]).astype(BF16)
            pairs = (
                (n_buf.at[a, :, pl.ds(k * KS, KS)], normed_s.at[place]),
                (h_buf.at[a, k, :, pl.ds(KT, KS)], raw_s.at[place]),
            )
            leaving.append([copy(p, q, out_sem.at[n, i]) for i, (p, q) in enumerate(pairs)])
            for c in leaving[n]:
                c.start()
        if a == 0 and not first:
            load.wait()
        nn = ((1,), (0,))
        for i, c in ((0, g), (1, 1 - g)):
            t = dot(t_buf[a], w_buf[a, i], nn)
            s = dot(n_buf[a], s_buf[a, i], nn)
            if a == 0 and first:
                acc[c, 0] = t
                acc[c, 1] = s
            else:
                acc[c, 0] += t
                acc[c, 1] += s
    store = copy(acc, logits, acc_sem)
    store.start()
    for copies in leaving:
        for c in copies:
            c.wait()
    store.wait()


def partial_logits(offsets, hidden, scales, gains, weights, before):
    first = before is None
    arrays = 2 * len(offsets)
    vmem = pl.BlockSpec(memory_space=pltpu.VMEM)
    hbm = pl.BlockSpec(memory_space=pl.ANY)
    out = pl.BlockSpec(memory_space=pltpu.HBM)
    operands = [*hidden, *scales, *gains, *weights]
    in_specs = [*[hbm] * arrays, *[vmem] * 4, *[hbm] * 4]
    aliases = {}
    if not first:
        aliases = {len(operands) + 1: 1, len(operands) + 2: 2}
        operands += before
        in_specs += [out] * 3
    return pl.pallas_call(
        functools.partial(logits_kernel, offsets, first),
        in_specs=in_specs,
        out_specs=[out] * 3,
        out_shape=[
            jax.ShapeDtypeStruct((2, 2, TOKENS, VOC), F32),
            jax.ShapeDtypeStruct((NTP, TOKENS, KS), BF16),
            jax.ShapeDtypeStruct((NTP, TOKENS, KS), BF16),
        ],
        scratch_shapes=[
            pltpu.VMEM((2, 2, TOKENS, VOC), F32),
            pltpu.VMEM((arrays, 2, TOKENS, KT + KS), BF16),
            pltpu.VMEM((arrays, 2, 2 * KT, VOC), BF16),
            pltpu.VMEM((arrays, 2, 2 * KS, VOC), BF16),
            pltpu.VMEM((arrays, TOKENS, 2 * KS), BF16),
            pltpu.VMEM((arrays, TOKENS, 2 * KT), BF16),
            pltpu.SemaphoreType.DMA((2 * arrays, 5)),
            pltpu.SemaphoreType.DMA((2 * arrays, 2)),
            pltpu.SemaphoreType.DMA,
        ],
        input_output_aliases=aliases,
        cost_estimate=pl.CostEstimate(
            flops=4 * arrays * TOKENS * 2 * VOC * (KT + KS),
            bytes_accessed=arrays * 2_400_000,
            transcendentals=0,
        ),
        compiler_params=params(WIDE_LIMIT),
    )(*operands)


def onehot_of(targets, base):
    spread = jnp.broadcast_to(targets.astype(F32), (128, TOKENS))
    targets = jnp.transpose(spread)[:, 0:1].astype(jnp.int32)
    lane = lax.broadcasted_iota(jnp.int32, (TOKENS, 2 * VOC), 1)
    column = jnp.where(lane < VOC, base[0] + lane, base[1] + lane - VOC)
    return column == targets


def stats_kernel(base, mine, other, targets, both, records):
    t, s = (
        jnp.concatenate([mine[0, i] + other[0, i], mine[1, i] + other[1, i]], axis=1)
        for i in range(2)
    )
    both[0] = t
    both[1] = s

    def row_sum(v):
        return jnp.sum(v, axis=1, keepdims=True)

    m_t = jnp.max(t, axis=1, keepdims=True)
    m_s = jnp.max(s, axis=1, keepdims=True)
    e_t = jnp.exp(t - m_t)
    hit = onehot_of(targets[...], base)
    columns = [
        m_t, row_sum(e_t), row_sum(e_t * (t - s)), m_s, row_sum(jnp.exp(s - m_s)),
        row_sum(jnp.where(hit, s, 0.0)),
    ]
    lane = lax.broadcasted_iota(jnp.int32, (TOKENS, 128), 1)
    packed = jnp.zeros((TOKENS, 128), F32)
    for k, column in enumerate(columns):
        packed = jnp.where(lane == k, column, packed)
    rows = jnp.transpose(packed)[:8]
    for k in range(NTP):
        records[k] = rows


def local_stats(base, mine, other, targets):
    vmem = pl.BlockSpec(memory_space=pltpu.VMEM)
    return pl.pallas_call(
        stats_kernel,
        in_specs=[pl.BlockSpec(memory_space=pltpu.SMEM), vmem, vmem, vmem],
        out_specs=[vmem, vmem],
        out_shape=[
            jax.ShapeDtypeStruct((2, TOKENS, 2 * VOC), F32),
            jax.ShapeDtypeStruct((NTP, 8, TOKENS), F32),
        ],
        compiler_params=params(),
    )(base, mine, other, targets)


def merged(records):
    m_t, z_t, a, m_s, z_s, hit = (records[:, k, :] for k in range(6))
    top_t = jnp.max(m_t, axis=0, keepdims=True)
    top_s = jnp.max(m_s, axis=0, keepdims=True)
    w_t = jnp.exp(m_t - top_t)
    w_s = jnp.exp(m_s - top_s)

    def total(v):
        return jnp.sum(v, axis=0, keepdims=True)

    return top_t, total(w_t * z_t), total(w_t * a), top_s, total(w_s * z_s), total(hit)


def merge_kernel(copies, records, out):
    rows = merged(records[...])
    for c in range(copies):
        for k in range(6):
            out[c, k : k + 1, :] = rows[k]
        out[c, 6:8, :] = jnp.zeros((2, TOKENS), F32)


def merge_records(records, copies):
    vmem = pl.BlockSpec(memory_space=pltpu.VMEM)
    return pl.pallas_call(
        functools.partial(merge_kernel, copies),
        in_specs=[vmem],
        out_specs=vmem,
        out_shape=jax.ShapeDtypeStruct((copies, 8, TOKENS), F32),
        compiler_params=params(),
    )(records)


def grad_kernel(
    base, records, both, targets, r_s, raw_s, s_own, s_oth, out, grad_own, loss, grads, gains, parts, sems
):
    j = pl.program_id(0)
    g = base[2]

    @pl.when(j == 0)
    def _():
        top_t, z_t, a, top_s, z_s, hit = merged(records[...])
        lse_t = top_t + jnp.log(z_t)
        lse_s = top_s + jnp.log(z_s)
        loss[...] = a / z_t - lse_t + lse_s + ALPHA * (lse_s - hit)
        row = lax.broadcasted_iota(jnp.int32, (128, TOKENS), 0)
        packed = jnp.where(row == 0, lse_t, jnp.where(row == 1, lse_s, 0.0))
        columns = jnp.transpose(packed)
        p_t = jnp.exp(both[0] - columns[:, 0:1])
        p_s = jnp.exp(both[1] - columns[:, 1:2])
        hits = onehot_of(targets[...], base).astype(F32)
        grad = (LOSS_SCALE * ((1.0 + ALPHA) * p_s - p_t - ALPHA * hits)).astype(BF16)
        grads[0] = grad[:, :VOC]
        grads[1] = grad[:, VOC:]
        grad_own[...] = grads[g]

    nt = ((1,), (1,))
    wide = (4 * KS, VOC)
    part = dot(grads[g], s_own[...].reshape(wide), nt) + dot(grads[1 - g], s_oth[...].reshape(wide), nt)
    for k in range(4):
        piece = part[:, k * KS : (k + 1) * KS]
        rows = pl.ds(pl.multiple_of((j * 4 + k) * 16, 16), 16)
        parts[:, rows, :] = piece.astype(BF16).reshape(NTP, 16, KS)
        xhat = raw_s[k].astype(F32) * r_s[...]
        gains[pl.ds(j * 4 + k, 1), :] = jnp.sum(piece * xhat, axis=0, keepdims=True)

    def leave(n, count):
        rows = pl.ds(pl.multiple_of(n * 64, 64), count)
        return pltpu.make_async_copy(parts.at[:, rows, :], out.at[:, rows, :], sems.at[n])

    leave(j, 64).start()

    @pl.when(j == 3)
    def _():
        gain = gains[...]
        high = gain.astype(BF16)
        low = (gain - high.astype(F32)).astype(BF16)
        for c in range(NTP):
            parts[c, 256:272, :] = high
            parts[c, 272:288, :] = low
        leave(4, 32).start()
        for n in range(4):
            leave(n, 64).wait()
        leave(4, 32).wait()


def grad_parts(base, records, both, targets, r_s, raw_s, s_own, s_oth):
    whole = lambda *shape: pl.BlockSpec(shape, lambda j, b: (0,) * len(shape))
    grid_spec = pltpu.PrefetchScalarGridSpec(
        num_scalar_prefetch=1,
        grid=(4,),
        in_specs=[
            whole(NZ, 8, TOKENS), whole(2, TOKENS, 2 * VOC), whole(1, TOKENS), whole(TOKENS, 1),
            pl.BlockSpec((4, TOKENS, KS), lambda j, b: (j, 0, 0)),
            pl.BlockSpec((4, KS, VOC), lambda j, b: (j, 0, 0)),
            pl.BlockSpec((4, 1, KS, VOC), lambda j, b: (j, b[2], 0, 0)),
        ],
        out_specs=[
            pl.BlockSpec(memory_space=pltpu.HBM), whole(TOKENS, VOC), whole(1, TOKENS),
        ],
        scratch_shapes=[
            pltpu.VMEM((2, TOKENS, VOC), BF16),
            pltpu.VMEM((NTP, KS), F32),
            pltpu.VMEM((NTP, 288, KS), BF16),
            pltpu.SemaphoreType.DMA((5,)),
        ],
    )
    return pl.pallas_call(
        grad_kernel,
        grid_spec=grid_spec,
        out_shape=[
            jax.ShapeDtypeStruct((NTP, 288, KS), BF16),
            jax.ShapeDtypeStruct((TOKENS, VOC), BF16),
            jax.ShapeDtypeStruct((1, TOKENS), F32),
        ],
        compiler_params=params(),
    )(base, records, both, targets, r_s, raw_s, s_own, s_oth)


def head_kernel(base, mine, other, grad, out):
    g = base[2]
    tn = ((0,), (0,))
    for k in range(4):
        out[k, g] = dot(mine[k], grad[...], tn).astype(BF16)
        out[k, 1 - g] = dot(other[k], grad[...], tn).astype(BF16)


def head_gradient(base, mine, other, grad):
    block = pl.BlockSpec((4, TOKENS, KS), lambda j, b: (j, 0, 0))
    grid_spec = pltpu.PrefetchScalarGridSpec(
        num_scalar_prefetch=1,
        grid=(4,),
        in_specs=[block, block, pl.BlockSpec((TOKENS, VOC), lambda j, b: (0, 0))],
        out_specs=pl.BlockSpec((4, 2, KS, VOC), lambda j, b: (j, 0, 0, 0)),
    )
    return pl.pallas_call(
        head_kernel,
        grid_spec=grid_spec,
        out_shape=jax.ShapeDtypeStruct((NTP, 2, KS, VOC), BF16),
        cost_estimate=pl.CostEstimate(
            flops=2 * NTP * 2 * KS * TOKENS * VOC, bytes_accessed=4_500_000, transcendentals=0
        ),
        compiler_params=params(),
    )(base, mine, other, grad)


def fold_kernel(parts, out, total):
    acc = parts[0].astype(F32)
    for k in range(1, NTP):
        acc = acc + parts[k].astype(F32)
    total[...] = acc
    gain = total[256:272, :] + total[272:288, :]
    for z in range(NZ):
        for i in range(2):
            out[z, i * 16 : (i + 1) * 16, :] = total[pl.ds(2 * z + i, 16, stride=16), :]
        out[z, 32:48, :] = gain


def fold_parts(parts):
    vmem = pl.BlockSpec(memory_space=pltpu.VMEM)
    return pl.pallas_call(
        fold_kernel,
        in_specs=[vmem],
        out_specs=vmem,
        out_shape=jax.ShapeDtypeStruct((NZ, 48, KS), F32),
        scratch_shapes=[pltpu.VMEM((288, KS), F32)],
        compiler_params=params(),
    )(parts)


def sum_kernel(parts, rows, out):
    acc = parts[0]
    for k in range(1, NZ):
        acc = acc + parts[k]
    out[0:48, :] = acc
    out[48:80, :] = rows[...]


def sum_parts(parts, rows):
    vmem = pl.BlockSpec(memory_space=pltpu.VMEM)
    return pl.pallas_call(
        sum_kernel,
        in_specs=[vmem, vmem],
        out_specs=vmem,
        out_shape=jax.ShapeDtypeStruct((80, KS), F32),
        compiler_params=params(),
    )(parts, rows)


def final_kernel(mine, other, gain, hidden, gain_gradient, rows):
    g = lax.axis_index("grp")

    def all_features(v):
        return jnp.sum(v)

    halves = (mine, other)
    total = []
    for i in range(2):
        own_rows = slice(48 + 16 * i, 64 + 16 * i)
        squares = sum(all_features(h[own_rows, :] * h[own_rows, :]) for h in halves)
        scale = lax.rsqrt(jnp.full((1, 1), squares / (2 * NTP * KS) + EPS, F32))
        pairs = []
        for k, h in enumerate(halves):
            xhat = h[own_rows, :] * scale
            dy = h[16 * i : 16 * i + 16, :] * gain[g if k == 0 else 1 - g]
            pairs.append((xhat, dy))
        mean = sum(all_features(dy * xhat) for xhat, dy in pairs) / (2 * NTP * KS)
        total.append([scale * (dy - xhat * mean) for xhat, dy in pairs])
    for k, h in enumerate(halves):
        c = g if k == 0 else 1 - g
        for j in range(NTP):
            lanes = pl.ds(pl.multiple_of((2 * j + c) * KS, KS), KS)
            for i in range(2):
                rows[i : i + 1, lanes] = total[i][k][j : j + 1, :]
            gain_gradient[:, lanes] = h[32 + j : 33 + j, :]
    hidden[...] = rows[0:2, :].astype(BF16)


def norm_backward(mine, other, gain):
    vmem = pl.BlockSpec(memory_space=pltpu.VMEM)
    return pl.pallas_call(
        final_kernel,
        in_specs=[vmem] * 3,
        out_specs=[vmem] * 2,
        out_shape=[
            jax.ShapeDtypeStruct((2, 2 * NTP * KS), BF16),
            jax.ShapeDtypeStruct((1, 2 * NTP * KS), F32),
        ],
        scratch_shapes=[pltpu.VMEM((8, 2 * NTP * KS), F32)],
        compiler_params=params(),
    )(mine, other, gain)


def squares_kernel(slab, out):
    def lanes(low, high):
        total = 0.0
        for k in range(low, high, 128):
            v = slab[:, k : k + 128].astype(F32)
            total = total + v * v
        return jnp.sum(jnp.transpose(total), axis=0, keepdims=True)

    out[0:1, :] = lanes(0, KT)
    out[1:2, :] = lanes(KT, KT + KS)
    out[2:8, :] = jnp.zeros((6, TOKENS), F32)


def both_kernel(mine, other, out):
    total = mine[...] + other[...]
    for k in range(NTP):
        out[k] = total


def scales_kernel(widths, squares, r_t, r_s):
    total = jnp.sum(squares[...], axis=0)
    columns = jnp.transpose(
        jnp.concatenate(
            [lax.rsqrt(total[i : i + 1, :] / widths[i] + EPS) for i in range(2)]
            + [jnp.zeros((126, TOKENS), F32)],
            axis=0,
        )
    )
    r_t[...] = columns[:, 0:1]
    r_s[...] = columns[:, 1:2]


def small_call(kernel, shapes, *operands):
    vmem = pl.BlockSpec(memory_space=pltpu.VMEM)
    return pl.pallas_call(
        kernel,
        in_specs=[vmem] * len(operands),
        out_specs=[vmem] * len(shapes),
        out_shape=[jax.ShapeDtypeStruct(shape, F32) for shape in shapes],
        compiler_params=params(),
    )(*operands)


def on_device(
    teacher_hidden, teacher_gain, teacher_head, student_hidden, student_gain, student_head, targets
):
    g = lax.axis_index("grp")
    tp = lax.axis_index("tp")
    z = lax.axis_index("tok")

    w4 = teacher_head.reshape(NTP, 2, KT, VOC)
    s4 = student_head.reshape(NTP, 2, KS, VOC)
    w_oth, s_oth = swap_cores(w4), swap_cores(s4)

    block = jnp.concatenate(
        [
            lax.dynamic_slice_in_dim(teacher_hidden, g * KT, KT, 1),
            lax.dynamic_slice_in_dim(student_hidden, g * KS, KS, 1),
        ],
        axis=1,
    )
    slab = lax.all_to_all(
        jnp.broadcast_to(block[None], (NZ, *block.shape)), "tok", 0, 0, tiled=True
    ).reshape(TOKENS, KT + KS)
    w_own, s_own = bring_halves(w4, s4)
    gain_t, gain_s = teacher_gain.reshape(32, KT), student_gain.reshape(32, KS)
    slab, w_oth, s_oth, w_own, s_own, gain_t, gain_s = lax.optimization_barrier(
        (slab, w_oth, s_oth, w_own, s_own, gain_t, gain_s)
    )
    (half,) = small_call(squares_kernel, [(8, TOKENS)], slab)
    slab, half = lax.optimization_barrier((slab, half))
    half_oth = swap_cores(half)
    opposite = shift_first(slab, 2)
    slab, half_oth = lax.optimization_barrier((slab, half_oth))
    by_shift = [shift_first(slab, 1), opposite, shift_first(slab, 3)]
    (copies,) = small_call(both_kernel, [(NTP, 8, TOKENS)], half, half_oth)
    widths = (teacher_gain.shape[0], student_gain.shape[0])
    r_t, r_s = small_call(
        functools.partial(scales_kernel, widths),
        [(TOKENS, 1), (TOKENS, 1)],
        lax.all_to_all(copies, "tp", 0, 0, tiled=True),
    )
    low, high = jnp.stack([slab, by_shift[0]]), jnp.stack(by_shift[1:])
    low, high, r_t, r_s = lax.optimization_barrier((low, high, r_t, r_s))
    back_low = shift_second(low, 1)
    fore_high = shift_second(high, -1)
    back_high = shift_second(high, 1)
    fore_low = shift_second(low, -1)
    heads = functools.partial(
        partial_logits,
        scales=(r_t, r_s),
        gains=(gain_t, gain_s),
        weights=(w_own, w_oth, s_own, s_oth),
    )
    done = heads((0,), (low, high), before=None)
    *done, back_low, fore_high = lax.optimization_barrier((*done, back_low, fore_high))
    far_low = shift_second(back_low, 1)
    far_high = shift_second(fore_high, -1)
    done = heads((-1, 1), (back_low, back_high, fore_low, fore_high), before=done)
    half, normed_s, raw_s = heads((2,), (far_low, far_high), before=done)
    column = (tp * NZ + z) * VOC
    base = jnp.stack([column, NTP * NZ * VOC + column, g]).astype(jnp.int32)
    targets_row = targets[None, :]
    both, records = local_stats(base, half, swap_cores(half), targets_row)
    normed_oth = swap_cores(normed_s)
    records, normed_oth = lax.optimization_barrier((records, normed_oth))
    records = lax.all_to_all(records, "tp", 0, 0, tiled=True)
    records = lax.all_to_all(merge_records(records, NZ), "tok", 0, 0, tiled=True)
    parts, grad_own, loss = grad_parts(
        base, records, both, targets_row, r_s, raw_s, s_own, s_oth
    )
    arrived = lax.all_to_all(parts, "tp", 0, 0, tiled=True)
    d_head = head_gradient(base, normed_s, normed_oth, grad_own)
    arrived, d_head = lax.optimization_barrier((arrived, d_head))
    arrived = lax.all_to_all(fold_parts(arrived), "tok", 0, 0, tiled=True)
    hidden_rows = lax.dynamic_slice_in_dim(raw_s, tp * 16 + z * 2, 2, 1)
    hidden_rows = hidden_rows.astype(F32).transpose(1, 0, 2).reshape(32, KS)
    mine = sum_parts(arrived, hidden_rows)
    hidden_gradient, gain_gradient = norm_backward(
        mine, swap_cores(mine), student_gain.reshape(NTP, 2, KS).transpose(1, 0, 2)
    )
    return (
        loss.reshape(TOKENS),
        d_head.reshape(student_head.shape),
        hidden_gradient,
        gain_gradient.reshape(2 * NTP * KS),
    )


def solution(mesh):
    placed = (
        P("tok", "tp"),
        P(),
        P(None, ("grp", "tp", "tok")),
        P("tok", "tp"),
        P(),
        P(None, ("grp", "tp", "tok")),
        P(),
    )
    return jax.shard_map(
        on_device,
        mesh=mesh,
        in_specs=placed,
        out_specs=(P(), P(None, ("grp", "tp", "tok")), P(("tp", "tok"), None), P()),
        check_vma=False,
    )
```

```python
import functools

import jax
import jax.numpy as jnp
from jax import lax
from jax.experimental import pallas as pl
from jax.experimental.pallas import tpu as pltpu
from jax.sharding import PartitionSpec as P

EPS = 1e-05
ALPHA = 0.0625
LOSS_SCALE = 4096.0
AXES = ("grp", "tp", "tok")
F32 = jnp.float32
BF16 = jnp.bfloat16
VMEM_LIMIT = 16 * 1024 * 1024
WIDE_LIMIT = 20 * 1024 * 1024
NX, NY, NZ = 4, 4, 8
NTP = NX * NY
TOKENS = 256
KT = 512
KS = 128
VOC = 256


def permute(value, move):
    pairs = []
    for g in range(2):
        for x in range(NX):
            for y in range(NY):
                for z in range(NZ):
                    g2, x2, y2, z2 = move(g, x, y, z)
                    source = (g * NTP + x * NY + y) * NZ + z
                    target = ((g2 % 2) * NTP + (x2 % NX) * NY + y2 % NY) * NZ + z2 % NZ
                    pairs.append((source, target))
    return lax.ppermute(value, AXES, pairs)


def swap_cores(value):
    return permute(value, lambda g, x, y, z: (g + 1, x, y, z))


def shift_first(value, d):
    return permute(value, lambda g, x, y, z: (g, x, y + d, z) if g == 0 else (g, x + d, y, z))


def shift_second(value, d):
    return permute(value, lambda g, x, y, z: (g, x + d, y, z) if g == 0 else (g, x, y + d, z))


def params(limit=VMEM_LIMIT):
    return pltpu.CompilerParams(vmem_limit_bytes=limit)


def dot(a, b, dims):
    return lax.dot_general(a, b, (dims, ((), ())), preferred_element_type=F32)


def bring_kernel(w4, s4, w_own, s_own, sems):
    g = lax.axis_index("grp")
    copies = [
        pltpu.make_async_copy(source.at[:, g], target, sems.at[i])
        for i, (source, target) in enumerate(((w4, w_own), (s4, s_own)))
    ]
    for c in copies:
        c.start()
    for c in copies:
        c.wait()


def bring_halves(w4, s4):
    vmem = pl.BlockSpec(memory_space=pltpu.VMEM)
    hbm = pl.BlockSpec(memory_space=pl.ANY)
    return pl.pallas_call(
        bring_kernel,
        in_specs=[hbm, hbm],
        out_specs=[vmem, vmem],
        out_shape=[
            jax.ShapeDtypeStruct((NTP, KT, VOC), BF16),
            jax.ShapeDtypeStruct((NTP, KS, VOC), BF16),
        ],
        scratch_shapes=[pltpu.SemaphoreType.DMA((2,))],
        compiler_params=params(),
    )(w4, s4)


def logits_kernel(offsets, first, *refs):
    refs = list(refs)
    take = lambda n: [refs.pop(0) for _ in range(n)]
    arrays = 2 * len(offsets)
    hidden = take(arrays)
    r_t, r_s, gain_t, gain_s, w_own, w_oth, s_own, s_oth = take(8)
    before = None if first else take(3)[0]
    logits, normed_s, raw_s, acc, h_buf, w_buf, s_buf, n_buf, t_buf, in_sem, out_sem, acc_sem = refs
    g = lax.axis_index("grp")
    tp = lax.axis_index("tp")
    x, y = lax.div(tp, NY), lax.rem(tp, NY)
    position, line = jnp.where(g == 0, x, y), jnp.where(g == 0, y, x)
    copy = pltpu.make_async_copy
    if not first:
        load = copy(before, acc, acc_sem)
        load.start()
    places, arriving, leaving = [], [], []
    for a in range(arrays):
        ahead = lax.rem(position + offsets[a // 2] + NX, NX)
        for k in range(2):
            order = lax.rem(line - (2 * (a % 2) + k) + NX, NX)
            place = jnp.where(g == 0, ahead * NY + order, order * NY + ahead)
            places.append(place)
            t_rows, s_rows = pl.ds(k * KT, KT), pl.ds(k * KS, KS)
            sources = (
                (hidden[a].at[k], h_buf.at[a, k]),
                (w_own.at[place], w_buf.at[a, 0, t_rows]),
                (w_oth.at[place, g], w_buf.at[a, 1, t_rows]),
                (s_own.at[place], s_buf.at[a, 0, s_rows]),
                (s_oth.at[place, g], s_buf.at[a, 1, s_rows]),
            )
            n = 2 * a + k
            arriving.append([copy(p, q, in_sem.at[n, i]) for i, (p, q) in enumerate(sources)])
            for c in arriving[n]:
                c.start()
    for a in range(arrays):
        for k in range(2):
            n = 2 * a + k
            place = places[n]
            for c in arriving[n]:
                c.wait()
            row = pl.ds(place * 2 + g, 1)
            h_t = h_buf[a, k, :, :KT].astype(F32)
            t_buf[a, :, k * KT : (k + 1) * KT] = (h_t * r_t[...] * gain_t[row, :]).astype(BF16)
            h_s = h_buf[a, k, :, KT:].astype(F32)
            n_buf[a, :, k * KS : (k + 1) * KS] = (h_s * r_s[...] * gain_s[row, :]).astype(BF16)
            pairs = (
                (n_buf.at[a, :, pl.ds(k * KS, KS)], normed_s.at[place]),
                (h_buf.at[a, k, :, pl.ds(KT, KS)], raw_s.at[place]),
            )
            leaving.append([copy(p, q, out_sem.at[n, i]) for i, (p, q) in enumerate(pairs)])
            for c in leaving[n]:
                c.start()
        if a == 0 and not first:
            load.wait()
        nn = ((1,), (0,))
        for i, c in ((0, g), (1, 1 - g)):
            t = dot(t_buf[a], w_buf[a, i], nn)
            s = dot(n_buf[a], s_buf[a, i], nn)
            if a == 0 and first:
                acc[c, 0] = t
                acc[c, 1] = s
            else:
                acc[c, 0] += t
                acc[c, 1] += s
    store = copy(acc, logits, acc_sem)
    store.start()
    for copies in leaving:
        for c in copies:
            c.wait()
    store.wait()


def partial_logits(offsets, hidden, scales, gains, weights, before):
    first = before is None
    arrays = 2 * len(offsets)
    vmem = pl.BlockSpec(memory_space=pltpu.VMEM)
    hbm = pl.BlockSpec(memory_space=pl.ANY)
    out = pl.BlockSpec(memory_space=pltpu.HBM)
    operands = [*hidden, *scales, *gains, *weights]
    in_specs = [*[hbm] * arrays, *[vmem] * 4, *[hbm] * 4]
    aliases = {}
    if not first:
        aliases = {len(operands) + 1: 1, len(operands) + 2: 2}
        operands += before
        in_specs += [out] * 3
    return pl.pallas_call(
        functools.partial(logits_kernel, offsets, first),
        in_specs=in_specs,
        out_specs=[out] * 3,
        out_shape=[
            jax.ShapeDtypeStruct((2, 2, TOKENS, VOC), F32),
            jax.ShapeDtypeStruct((NTP, TOKENS, KS), BF16),
            jax.ShapeDtypeStruct((NTP, TOKENS, KS), BF16),
        ],
        scratch_shapes=[
            pltpu.VMEM((2, 2, TOKENS, VOC), F32),
            pltpu.VMEM((arrays, 2, TOKENS, KT + KS), BF16),
            pltpu.VMEM((arrays, 2, 2 * KT, VOC), BF16),
            pltpu.VMEM((arrays, 2, 2 * KS, VOC), BF16),
            pltpu.VMEM((arrays, TOKENS, 2 * KS), BF16),
            pltpu.VMEM((arrays, TOKENS, 2 * KT), BF16),
            pltpu.SemaphoreType.DMA((2 * arrays, 5)),
            pltpu.SemaphoreType.DMA((2 * arrays, 2)),
            pltpu.SemaphoreType.DMA,
        ],
        input_output_aliases=aliases,
        cost_estimate=pl.CostEstimate(
            flops=4 * arrays * TOKENS * 2 * VOC * (KT + KS),
            bytes_accessed=arrays * 2_400_000,
            transcendentals=0,
        ),
        compiler_params=params(WIDE_LIMIT),
    )(*operands)


def onehot_of(targets, base):
    spread = jnp.broadcast_to(targets.astype(F32), (128, TOKENS))
    targets = jnp.transpose(spread)[:, 0:1].astype(jnp.int32)
    lane = lax.broadcasted_iota(jnp.int32, (TOKENS, 2 * VOC), 1)
    column = jnp.where(lane < VOC, base[0] + lane, base[1] + lane - VOC)
    return column == targets


def stats_kernel(base, mine, other, targets, both, records):
    t, s = (
        jnp.concatenate([mine[0, i] + other[0, i], mine[1, i] + other[1, i]], axis=1)
        for i in range(2)
    )
    both[0] = t
    both[1] = s

    def row_sum(v):
        return jnp.sum(v, axis=1, keepdims=True)

    m_t = jnp.max(t, axis=1, keepdims=True)
    m_s = jnp.max(s, axis=1, keepdims=True)
    e_t = jnp.exp(t - m_t)
    hit = onehot_of(targets[...], base)
    columns = [
        m_t, row_sum(e_t), row_sum(e_t * (t - s)), m_s, row_sum(jnp.exp(s - m_s)),
        row_sum(jnp.where(hit, s, 0.0)),
    ]
    lane = lax.broadcasted_iota(jnp.int32, (TOKENS, 128), 1)
    packed = jnp.zeros((TOKENS, 128), F32)
    for k, column in enumerate(columns):
        packed = jnp.where(lane == k, column, packed)
    rows = jnp.transpose(packed)[:8]
    for k in range(NTP):
        records[k] = rows


def local_stats(base, mine, other, targets):
    vmem = pl.BlockSpec(memory_space=pltpu.VMEM)
    return pl.pallas_call(
        stats_kernel,
        in_specs=[pl.BlockSpec(memory_space=pltpu.SMEM), vmem, vmem, vmem],
        out_specs=[vmem, vmem],
        out_shape=[
            jax.ShapeDtypeStruct((2, TOKENS, 2 * VOC), F32),
            jax.ShapeDtypeStruct((NTP, 8, TOKENS), F32),
        ],
        compiler_params=params(),
    )(base, mine, other, targets)


def merged(records):
    m_t, z_t, a, m_s, z_s, hit = (records[:, k, :] for k in range(6))
    top_t = jnp.max(m_t, axis=0, keepdims=True)
    top_s = jnp.max(m_s, axis=0, keepdims=True)
    w_t = jnp.exp(m_t - top_t)
    w_s = jnp.exp(m_s - top_s)

    def total(v):
        return jnp.sum(v, axis=0, keepdims=True)

    return top_t, total(w_t * z_t), total(w_t * a), top_s, total(w_s * z_s), total(hit)


def merge_kernel(copies, records, out):
    rows = merged(records[...])
    for c in range(copies):
        for k in range(6):
            out[c, k : k + 1, :] = rows[k]
        out[c, 6:8, :] = jnp.zeros((2, TOKENS), F32)


def merge_records(records, copies):
    vmem = pl.BlockSpec(memory_space=pltpu.VMEM)
    return pl.pallas_call(
        functools.partial(merge_kernel, copies),
        in_specs=[vmem],
        out_specs=vmem,
        out_shape=jax.ShapeDtypeStruct((copies, 8, TOKENS), F32),
        compiler_params=params(),
    )(records)


def grad_kernel(
    base, records, both, targets, r_s, raw_s, s_own, s_oth, out, grad_own, loss, grads, gains, parts, sems
):
    j = pl.program_id(0)
    g = base[2]

    @pl.when(j == 0)
    def _():
        top_t, z_t, a, top_s, z_s, hit = merged(records[...])
        lse_t = top_t + jnp.log(z_t)
        lse_s = top_s + jnp.log(z_s)
        loss[...] = a / z_t - lse_t + lse_s + ALPHA * (lse_s - hit)
        row = lax.broadcasted_iota(jnp.int32, (128, TOKENS), 0)
        packed = jnp.where(row == 0, lse_t, jnp.where(row == 1, lse_s, 0.0))
        columns = jnp.transpose(packed)
        p_t = jnp.exp(both[0] - columns[:, 0:1])
        p_s = jnp.exp(both[1] - columns[:, 1:2])
        hits = onehot_of(targets[...], base).astype(F32)
        grad = (LOSS_SCALE * ((1.0 + ALPHA) * p_s - p_t - ALPHA * hits)).astype(BF16)
        grads[0] = grad[:, :VOC]
        grads[1] = grad[:, VOC:]
        grad_own[...] = grads[g]

    nt = ((1,), (1,))
    wide = (4 * KS, VOC)
    part = dot(grads[g], s_own[...].reshape(wide), nt) + dot(grads[1 - g], s_oth[...].reshape(wide), nt)
    for k in range(4):
        piece = part[:, k * KS : (k + 1) * KS]
        rows = pl.ds(pl.multiple_of((j * 4 + k) * 16, 16), 16)
        parts[:, rows, :] = piece.astype(BF16).reshape(NTP, 16, KS)
        xhat = raw_s[k].astype(F32) * r_s[...]
        gains[pl.ds(j * 4 + k, 1), :] = jnp.sum(piece * xhat, axis=0, keepdims=True)

    def leave(n, count):
        rows = pl.ds(pl.multiple_of(n * 64, 64), count)
        return pltpu.make_async_copy(parts.at[:, rows, :], out.at[:, rows, :], sems.at[n])

    leave(j, 64).start()

    @pl.when(j == 3)
    def _():
        gain = gains[...]
        high = gain.astype(BF16)
        low = (gain - high.astype(F32)).astype(BF16)
        for c in range(NTP):
            parts[c, 256:272, :] = high
            parts[c, 272:288, :] = low
        leave(4, 32).start()
        for n in range(4):
            leave(n, 64).wait()
        leave(4, 32).wait()


def grad_parts(base, records, both, targets, r_s, raw_s, s_own, s_oth):
    whole = lambda *shape: pl.BlockSpec(shape, lambda j, b: (0,) * len(shape))
    grid_spec = pltpu.PrefetchScalarGridSpec(
        num_scalar_prefetch=1,
        grid=(4,),
        in_specs=[
            whole(NZ, 8, TOKENS), whole(2, TOKENS, 2 * VOC), whole(1, TOKENS), whole(TOKENS, 1),
            pl.BlockSpec((4, TOKENS, KS), lambda j, b: (j, 0, 0)),
            pl.BlockSpec((4, KS, VOC), lambda j, b: (j, 0, 0)),
            pl.BlockSpec((4, 1, KS, VOC), lambda j, b: (j, b[2], 0, 0)),
        ],
        out_specs=[
            pl.BlockSpec(memory_space=pltpu.HBM), whole(TOKENS, VOC), whole(1, TOKENS),
        ],
        scratch_shapes=[
            pltpu.VMEM((2, TOKENS, VOC), BF16),
            pltpu.VMEM((NTP, KS), F32),
            pltpu.VMEM((NTP, 288, KS), BF16),
            pltpu.SemaphoreType.DMA((5,)),
        ],
    )
    return pl.pallas_call(
        grad_kernel,
        grid_spec=grid_spec,
        out_shape=[
            jax.ShapeDtypeStruct((NTP, 288, KS), BF16),
            jax.ShapeDtypeStruct((TOKENS, VOC), BF16),
            jax.ShapeDtypeStruct((1, TOKENS), F32),
        ],
        compiler_params=params(),
    )(base, records, both, targets, r_s, raw_s, s_own, s_oth)


def head_kernel(base, mine, other, grad, out):
    g = base[2]
    tn = ((0,), (0,))
    for k in range(4):
        out[k, g] = dot(mine[k], grad[...], tn).astype(BF16)
        out[k, 1 - g] = dot(other[k], grad[...], tn).astype(BF16)


def head_gradient(base, mine, other, grad):
    block = pl.BlockSpec((4, TOKENS, KS), lambda j, b: (j, 0, 0))
    grid_spec = pltpu.PrefetchScalarGridSpec(
        num_scalar_prefetch=1,
        grid=(4,),
        in_specs=[block, block, pl.BlockSpec((TOKENS, VOC), lambda j, b: (0, 0))],
        out_specs=pl.BlockSpec((4, 2, KS, VOC), lambda j, b: (j, 0, 0, 0)),
    )
    return pl.pallas_call(
        head_kernel,
        grid_spec=grid_spec,
        out_shape=jax.ShapeDtypeStruct((NTP, 2, KS, VOC), BF16),
        cost_estimate=pl.CostEstimate(
            flops=2 * NTP * 2 * KS * TOKENS * VOC, bytes_accessed=4_500_000, transcendentals=0
        ),
        compiler_params=params(),
    )(base, mine, other, grad)


def fold_kernel(parts, out, total):
    acc = parts[0].astype(F32)
    for k in range(1, NTP):
        acc = acc + parts[k].astype(F32)
    total[...] = acc
    gain = total[256:272, :] + total[272:288, :]
    for z in range(NZ):
        for i in range(2):
            out[z, i * 16 : (i + 1) * 16, :] = total[pl.ds(2 * z + i, 16, stride=16), :]
        out[z, 32:48, :] = gain


def fold_parts(parts):
    vmem = pl.BlockSpec(memory_space=pltpu.VMEM)
    return pl.pallas_call(
        fold_kernel,
        in_specs=[vmem],
        out_specs=vmem,
        out_shape=jax.ShapeDtypeStruct((NZ, 48, KS), F32),
        scratch_shapes=[pltpu.VMEM((288, KS), F32)],
        compiler_params=params(),
    )(parts)


def sum_kernel(parts, rows, out):
    acc = parts[0]
    for k in range(1, NZ):
        acc = acc + parts[k]
    out[0:48, :] = acc
    out[48:80, :] = rows[...]


def sum_parts(parts, rows):
    vmem = pl.BlockSpec(memory_space=pltpu.VMEM)
    return pl.pallas_call(
        sum_kernel,
        in_specs=[vmem, vmem],
        out_specs=vmem,
        out_shape=jax.ShapeDtypeStruct((80, KS), F32),
        compiler_params=params(),
    )(parts, rows)


def final_kernel(mine, other, gain, hidden, gain_gradient, rows):
    g = lax.axis_index("grp")

    def all_features(v):
        return jnp.sum(v)

    halves = (mine, other)
    total = []
    for i in range(2):
        own_rows = slice(48 + 16 * i, 64 + 16 * i)
        squares = sum(all_features(h[own_rows, :] * h[own_rows, :]) for h in halves)
        scale = lax.rsqrt(jnp.full((1, 1), squares / (2 * NTP * KS) + EPS, F32))
        pairs = []
        for k, h in enumerate(halves):
            xhat = h[own_rows, :] * scale
            dy = h[16 * i : 16 * i + 16, :] * gain[g if k == 0 else 1 - g]
            pairs.append((xhat, dy))
        mean = sum(all_features(dy * xhat) for xhat, dy in pairs) / (2 * NTP * KS)
        total.append([scale * (dy - xhat * mean) for xhat, dy in pairs])
    for k, h in enumerate(halves):
        c = g if k == 0 else 1 - g
        for j in range(NTP):
            lanes = pl.ds(pl.multiple_of((2 * j + c) * KS, KS), KS)
            for i in range(2):
                rows[i : i + 1, lanes] = total[i][k][j : j + 1, :]
            gain_gradient[:, lanes] = h[32 + j : 33 + j, :]
    hidden[...] = rows[0:2, :].astype(BF16)


def norm_backward(mine, other, gain):
    vmem = pl.BlockSpec(memory_space=pltpu.VMEM)
    return pl.pallas_call(
        final_kernel,
        in_specs=[vmem] * 3,
        out_specs=[vmem] * 2,
        out_shape=[
            jax.ShapeDtypeStruct((2, 2 * NTP * KS), BF16),
            jax.ShapeDtypeStruct((1, 2 * NTP * KS), F32),
        ],
        scratch_shapes=[pltpu.VMEM((8, 2 * NTP * KS), F32)],
        compiler_params=params(),
    )(mine, other, gain)


def squares_kernel(slab, out):
    def lanes(low, high):
        total = 0.0
        for k in range(low, high, 128):
            v = slab[:, k : k + 128].astype(F32)
            total = total + v * v
        return jnp.sum(jnp.transpose(total), axis=0, keepdims=True)

    out[0:1, :] = lanes(0, KT)
    out[1:2, :] = lanes(KT, KT + KS)
    out[2:8, :] = jnp.zeros((6, TOKENS), F32)


def both_kernel(mine, other, out):
    total = mine[...] + other[...]
    for k in range(NTP):
        out[k] = total


def scales_kernel(widths, squares, r_t, r_s):
    total = jnp.sum(squares[...], axis=0)
    columns = jnp.transpose(
        jnp.concatenate(
            [lax.rsqrt(total[i : i + 1, :] / widths[i] + EPS) for i in range(2)]
            + [jnp.zeros((126, TOKENS), F32)],
            axis=0,
        )
    )
    r_t[...] = columns[:, 0:1]
    r_s[...] = columns[:, 1:2]


def small_call(kernel, shapes, *operands):
    vmem = pl.BlockSpec(memory_space=pltpu.VMEM)
    return pl.pallas_call(
        kernel,
        in_specs=[vmem] * len(operands),
        out_specs=[vmem] * len(shapes),
        out_shape=[jax.ShapeDtypeStruct(shape, F32) for shape in shapes],
        compiler_params=params(),
    )(*operands)


def on_device(
    teacher_hidden, teacher_gain, teacher_head, student_hidden, student_gain, student_head, targets
):
    g = lax.axis_index("grp")
    tp = lax.axis_index("tp")
    z = lax.axis_index("tok")

    w4 = teacher_head.reshape(NTP, 2, KT, VOC)
    s4 = student_head.reshape(NTP, 2, KS, VOC)
    w_oth, s_oth = swap_cores(w4), swap_cores(s4)

    block = jnp.concatenate(
        [
            lax.dynamic_slice_in_dim(teacher_hidden, g * KT, KT, 1),
            lax.dynamic_slice_in_dim(student_hidden, g * KS, KS, 1),
        ],
        axis=1,
    )
    slab = lax.all_to_all(
        jnp.broadcast_to(block[None], (NZ, *block.shape)), "tok", 0, 0, tiled=True
    ).reshape(TOKENS, KT + KS)
    w_own, s_own = bring_halves(w4, s4)
    gain_t, gain_s = teacher_gain.reshape(32, KT), student_gain.reshape(32, KS)
    slab, w_oth, s_oth, w_own, s_own, gain_t, gain_s = lax.optimization_barrier(
        (slab, w_oth, s_oth, w_own, s_own, gain_t, gain_s)
    )
    (half,) = small_call(squares_kernel, [(8, TOKENS)], slab)
    slab, half = lax.optimization_barrier((slab, half))
    half_oth = swap_cores(half)
    opposite = shift_first(slab, 2)
    slab, half_oth = lax.optimization_barrier((slab, half_oth))
    by_shift = [shift_first(slab, 1), opposite, shift_first(slab, 3)]
    (copies,) = small_call(both_kernel, [(NTP, 8, TOKENS)], half, half_oth)
    widths = (teacher_gain.shape[0], student_gain.shape[0])
    r_t, r_s = small_call(
        functools.partial(scales_kernel, widths),
        [(TOKENS, 1), (TOKENS, 1)],
        lax.all_to_all(copies, "tp", 0, 0, tiled=True),
    )
    low, high = jnp.stack([slab, by_shift[0]]), jnp.stack(by_shift[1:])
    low, high, r_t, r_s = lax.optimization_barrier((low, high, r_t, r_s))
    back_low = shift_second(low, 1)
    fore_high = shift_second(high, -1)
    back_high = shift_second(high, 1)
    fore_low = shift_second(low, -1)
    heads = functools.partial(
        partial_logits,
        scales=(r_t, r_s),
        gains=(gain_t, gain_s),
        weights=(w_own, w_oth, s_own, s_oth),
    )
    done = heads((0,), (low, high), before=None)
    *done, back_low, fore_high = lax.optimization_barrier((*done, back_low, fore_high))
    far_low = shift_second(back_low, 1)
    far_high = shift_second(fore_high, -1)
    done = heads((-1, 1), (back_low, back_high, fore_low, fore_high), before=done)
    half, normed_s, raw_s = heads((2,), (far_low, far_high), before=done)
    column = (tp * NZ + z) * VOC
    base = jnp.stack([column, NTP * NZ * VOC + column, g]).astype(jnp.int32)
    targets_row = targets[None, :]
    both, records = local_stats(base, half, swap_cores(half), targets_row)
    normed_oth = swap_cores(normed_s)
    hidden_rows = lax.dynamic_slice_in_dim(raw_s, tp * 16 + z * 2, 2, 1)
    hidden_rows = hidden_rows.astype(F32).transpose(1, 0, 2).reshape(32, KS)
    records, normed_oth, hidden_rows = lax.optimization_barrier((records, normed_oth, hidden_rows))
    records = lax.all_to_all(records, "tp", 0, 0, tiled=True)
    records = lax.all_to_all(merge_records(records, NZ), "tok", 0, 0, tiled=True)
    parts, grad_own, loss = grad_parts(
        base, records, both, targets_row, r_s, raw_s, s_own, s_oth
    )
    arrived = lax.all_to_all(parts, "tp", 0, 0, tiled=True)
    d_head = head_gradient(base, normed_s, normed_oth, grad_own)
    arrived, d_head = lax.optimization_barrier((arrived, d_head))
    arrived = lax.all_to_all(fold_parts(arrived), "tok", 0, 0, tiled=True)
    mine = sum_parts(arrived, hidden_rows)
    hidden_gradient, gain_gradient = norm_backward(
        mine, swap_cores(mine), student_gain.reshape(NTP, 2, KS).transpose(1, 0, 2)
    )
    return (
        loss.reshape(TOKENS),
        d_head.reshape(student_head.shape),
        hidden_gradient,
        gain_gradient.reshape(2 * NTP * KS),
    )


def solution(mesh):
    placed = (
        P("tok", "tp"),
        P(),
        P(None, ("grp", "tp", "tok")),
        P("tok", "tp"),
        P(),
        P(None, ("grp", "tp", "tok")),
        P(),
    )
    return jax.shard_map(
        on_device,
        mesh=mesh,
        in_specs=placed,
        out_specs=(P(), P(None, ("grp", "tp", "tok")), P(("tp", "tok"), None), P()),
        check_vma=False,
    )
```
